256 devices in a mesh: blk: 32 (over z, y_hi, core), rep: 8 (over y_lo, x).
Axes of the slice: x: 4, y: 4 (y_hi: 2, y_lo: 2; y = y_hi * 2 + y_lo), z: 8, core: 2. Of those that a mesh axis runs over, the one named last changes fastest.
Arguments:
- features: bfloat16 [65536, 128], P(('blk', 'rep')), may hold values from -6 to 6
- adj_tiles: bfloat16 [32, 8, 32, 8, 128, 128], P('blk', 'rep'), may hold values from -0.0625 to 0.0625
- tile_counts: int32 [32, 8, 32], P('blk', 'rep'), may hold values from 1 to 8
- dst_tile: int32 [32, 8, 32, 8], P('blk', 'rep'), may hold values from 0 to 15
- src_tile: int32 [32, 8, 32, 8], P('blk', 'rep'), may hold values from 0 to 1
- weight: float32 [128, 128], replicated, may hold values from -0.5 to 0.5
- bias_term: float32 [128], replicated, may hold values from -3 to 3
- cotangent: float32 [65536, 128], P(('blk', 'rep')), may hold values from -6 to 6
Outputs:
- activations: float32 [65536, 128], P(('blk', 'rep'))
- feature_grad: float32 [65536, 128], P(('blk', 'rep'))
- weight_grad: float32 [128, 128], replicated
The draws below stay inside these ranges and needn't reach their ends.
All inputs are finite; a program needn't handle non-finite values.
Results may differ from the reference program's by a relative error of at most 0.0029.
Values may be sent and summed in bfloat16 or wider, within the bound.
A program may use at most 64 MiB of HBM per device.

```python
import math
import jax
import jax.numpy as jnp
from jax import lax

FEAT = 128
TILE = 128
SHARD_TILES = 2
CAP = 8
NODES = 65536
N_BLK = 32
N_REP = 8


def draw_tile_counts(key, part):
    key = jax.random.fold_in(key, 11)
    level_key, count_key = jax.random.split(key)
    levels = jax.random.randint(level_key, (N_BLK, 1, 1), CAP // 2, CAP + 1)
    counts = jax.random.randint(count_key, (N_BLK, N_REP, N_BLK), 1, levels + 1)
    counts = counts.at[:, :, 0].set(CAP)
    return counts.astype(jnp.int32)


def place_ends(values, stream_key, low, high):
    longest = values.shape.index(max(values.shape))
    spots = []
    for shift in (0, 1):
        where = [jax.random.randint(jax.random.fold_in(stream_key, axis), (), 0, length) for axis, length in enumerate(values.shape)]
        where[longest] = (where[longest] + shift) % values.shape[longest]
        spots.append(tuple(where))
    return values.at[spots[0]].set(low).at[spots[1]].set(high)


def shard_levels(stream_key, extent, pieces, smallest, largest):
    gain, own = 1.0, jax.random.fold_in(stream_key, 6)
    for position, shards_of in pieces:
        steps = jnp.exp(jax.random.uniform(jax.random.fold_in(own, position), (shards_of,), jnp.float32, smallest / len(pieces), largest / len(pieces)))
        gain = gain * jnp.repeat(steps, extent[position] // shards_of).reshape([-1 if axis == position else 1 for axis in range(len(extent))])
    return gain


def bell_draw(key, shape, width, reach, cuts=(), dtype=jnp.bfloat16):
    values = jax.random.normal(key, shape, jnp.float32) * width
    if len(cuts) > 0:
        values = shard_levels(key, shape, cuts, -0.22, 0.18) * values
    return jnp.clip(values, min=-reach, max=reach).astype(dtype)


def setup_inputs(seed: int = 0) -> dict:
    seeds = jax.random.split(jax.random.key(seed), 9)
    return {
        "features": bell_draw(seeds[0], (NODES, FEAT), 1.0, 6.0, ((0, 256),)),
        "adj_tiles": bell_draw(seeds[1], (N_BLK, N_REP, N_BLK, CAP, TILE, TILE), (TILE * CAP * N_BLK // (2 * SHARD_TILES)) ** -0.5, 0.0625, ((0, 32), (1, 8))),
        "tile_counts": draw_tile_counts(jax.random.fold_in(seeds[8], 71), 0),
        "dst_tile": place_ends(jax.random.randint(seeds[3], (N_BLK, N_REP, N_BLK, CAP), 0, SHARD_TILES * N_REP), jax.random.fold_in(seeds[3], 1), 0, (SHARD_TILES * N_REP) - 1).astype(jnp.int32),
        "src_tile": place_ends(jax.random.randint(seeds[4], (N_BLK, N_REP, N_BLK, CAP), 0, SHARD_TILES), jax.random.fold_in(seeds[4], 1), 0, SHARD_TILES - 1).astype(jnp.int32),
        "weight": bell_draw(seeds[5], (FEAT, FEAT), FEAT ** -0.5, 0.5, (), jnp.float32),
        "bias_term": bell_draw(seeds[6], (FEAT,), 0.5, 3.0, (), jnp.float32),
        "cotangent": bell_draw(seeds[7], (NODES, FEAT), 1.0, 6.0, ((0, 256),), jnp.float32),
    }


def reference(features, adj_tiles, tile_counts, dst_tile, src_tile, weight, bias_term, cotangent):
    blocks = N_BLK
    group_size = N_REP
    block_tiles = SHARD_TILES * group_size
    shards = features.reshape(blocks, group_size, SHARD_TILES, TILE, FEAT)
    step_ids = jnp.arange(blocks).astype(jnp.int32)
    slot_ids = jnp.arange(CAP).astype(jnp.int32)

    def forward_block(b):
        source_blocks = ((b - step_ids) % blocks).astype(jnp.int32)

        def rep_terms(r):
            own_tiles = adj_tiles[b, r].astype(jnp.float32)
            live_mask = (slot_ids[None, :] < tile_counts[b, r][:, None]).astype(jnp.float32)
            sources = shards[source_blocks, r]
            picked = jax.vmap(lambda blk_rows, ids: blk_rows[ids])(sources, src_tile[b, r])
            product = jnp.einsum('sktu,skuf->sktf', own_tiles, picked.astype(jnp.float32)) * live_mask[:, :, None, None]
            summed = jnp.zeros((block_tiles, TILE, FEAT), jnp.float32)
            return summed.at[dst_tile[b, r].reshape(-1)].add(product.reshape(-1, TILE, FEAT))
        return lax.optimization_barrier(jnp.sum(lax.map(rep_terms, jnp.arange(group_size).astype(jnp.int32)), axis=0))
    aggregate = lax.map(forward_block, jnp.arange(blocks).astype(jnp.int32)).reshape(-1, FEAT)
    pre_act = jnp.dot(aggregate, weight, precision=lax.Precision.HIGHEST) + bias_term
    activations = jax.nn.silu(pre_act)
    sigmoid_val = jax.nn.sigmoid(pre_act)
    pre_grad = cotangent * sigmoid_val * (1.0 + pre_act * (1.0 - sigmoid_val))
    weight_grad = jnp.dot(aggregate.T, pre_grad, precision=lax.Precision.HIGHEST) / math.sqrt(NODES)
    agg_grad = jnp.dot(pre_grad, weight.T, precision=lax.Precision.HIGHEST).astype(jnp.bfloat16)
    block_grad = agg_grad.reshape(blocks, block_tiles, TILE, FEAT)

    def backward_block(grads, b):
        source_blocks = ((b - step_ids) % blocks).astype(jnp.int32)

        def rep_terms(r):
            own_tiles = adj_tiles[b, r].astype(jnp.float32)
            live_mask = (slot_ids[None, :] < tile_counts[b, r][:, None]).astype(jnp.float32)
            rows_sel = block_grad[b][dst_tile[b, r]].astype(jnp.float32)
            product = jnp.einsum('sktu,sktf->skuf', own_tiles, rows_sel) * live_mask[:, :, None, None]
            summed = jnp.zeros((blocks, SHARD_TILES, TILE, FEAT), jnp.float32)
            return summed.at[step_ids[:, None], src_tile[b, r]].add(product)
        terms = lax.map(rep_terms, jnp.arange(group_size).astype(jnp.int32))
        return (grads.at[source_blocks].add(jnp.swapaxes(terms, 0, 1)), None)
    start_grads = jnp.zeros((blocks, group_size, SHARD_TILES, TILE, FEAT), jnp.float32)
    feature_grad, unused_out = lax.scan(backward_block, start_grads, jnp.arange(blocks).astype(jnp.int32))
    return (activations, feature_grad.reshape(-1, FEAT), weight_grad)
```

```python
import functools
import math

import jax
import jax.numpy as jnp
from jax import lax
from jax.experimental import pallas as pl
from jax.experimental.pallas import tpu as pltpu
from jax.sharding import PartitionSpec as P

MESH = pl.DeviceIdType.MESH
F32 = jnp.float32
BF16 = jnp.bfloat16
HIGHEST = lax.Precision.HIGHEST


def kernel(
    blocks, reps, node_total,
    features, tiles_hbm, counts, dst, src, dst_vec, weight, bias, cotangent,
    act_out, grad_out, wgrad_out,
    tiles, feats, chain, links_vec, links,
    part, part_in, grads_t, wterm, wrep, wquad, wz, wall,
    sib_out, sib_in, own_sum, z_in, y_in,
    tile_sem, link_sem, ag_send, ag_recv, rs_send, rs_recv, g_send, g_recv,
    w_send, w1_recv, w2_recv, w3_recv, w4_recv,
    sib_send, sib_recv, z_send, z_recv, y_send, y_recv,
):
    nz = blocks // 4
    half = nz // 2
    cap = dst.shape[1]
    tile = tiles.shape[1]
    feat = features.shape[1]
    n_slots = blocks * cap
    b = lax.axis_index("blk")
    r = lax.axis_index("rep")
    core = lax.rem(b, 2)
    yh = lax.rem(b // 2, 2)
    z = b // 4
    sib = b + 1 - 2 * core
    partner = b + 2 - 4 * yh
    diag = sib + 2 - 4 * yh
    up = lax.rem(b + 4, blocks)
    down = lax.rem(b + blocks - 4, blocks)

    sent = []

    def send(src_ref, dst_ref, send_sem, recv_sem, blk, rep):
        copy = pltpu.make_async_remote_copy(
            src_ref=src_ref, dst_ref=dst_ref, send_sem=send_sem, recv_sem=recv_sem,
            device_id=(blk, rep), device_id_type=MESH,
        )
        copy.start()
        sent.append(copy)

    def arrived(dst_ref, recv_sem):
        pltpu.make_async_remote_copy(
            src_ref=dst_ref, dst_ref=dst_ref, send_sem=w_send.at[0], recv_sem=recv_sem,
            device_id=(sib, r), device_id_type=MESH,
        ).wait_recv()

    tile_copy = pltpu.make_async_copy(tiles_hbm, tiles, tile_sem)
    tile_copy.start()

    z_peers = [lax.rem(b + 4 * i, blocks) for i in range(1, nz)]
    rep_peers = [lax.rem(r + i, reps) for i in range(1, reps)]
    barrier = pltpu.get_barrier_semaphore()
    for blk in [sib, partner, diag] + z_peers:
        pl.semaphore_signal(barrier, inc=1, device_id=(blk, r), device_id_type=MESH)
    for rep in rep_peers:
        pl.semaphore_signal(barrier, inc=1, device_id=(b, rep), device_id_type=MESH)
    feats[b] = features[...]
    pl.semaphore_wait(barrier, 3 + len(z_peers) + len(rep_peers))

    ag_count = [0]

    def pass_on(u, targets):
        for blk in targets:
            send(feats.at[u], feats.at[u], ag_send.at[ag_count[0]], ag_recv.at[u], blk, r)
            ag_count[0] += 1

    pass_on(b, [partner, up, down, sib])

    def step_of(n):
        group, j = n // 4, lax.rem(n, 4)
        dist = (group + 1) // 2
        zoff = lax.rem(jnp.where(lax.rem(group, 2) == 1, nz - dist, dist), nz)
        return lax.rem(z + zoff, nz) * 4 + j

    dst_tab = dst_vec[...]
    slot_iota = lax.broadcasted_iota(jnp.int32, dst_tab.shape, 0) * cap + lax.broadcasted_iota(
        jnp.int32, dst_tab.shape, 1
    )
    tile_iota = lax.broadcasted_iota(jnp.int32, (8, 128), 1)

    def link_step(n, carry):
        current, before, last = carry
        s = lax.rem(b - step_of(n) + blocks, blocks)
        for k in range(cap):
            to = jnp.where(k < counts[s], dst[s, k], -1)
            before = jnp.where(slot_iota == s * cap + k, current, before)
            current = jnp.where(dst_tab == to, n * cap + k, current)
            last = jnp.where(tile_iota == to, n * cap + k, last)
        return current, before, last

    nothing = jnp.full(dst_tab.shape, n_slots, jnp.int32)
    current, before, last = lax.fori_loop(
        0, blocks, link_step, (nothing, nothing, jnp.full((8, 128), n_slots, jnp.int32))
    )
    links_vec[...] = jnp.zeros(links_vec.shape, jnp.int32)
    links_vec[0:blocks, 0:cap] = before
    links_vec[blocks:blocks + 8, :] = last
    link_copy = pltpu.make_async_copy(links_vec, links, link_sem)
    link_copy.start()
    chain[n_slots] = jnp.zeros((tile, feat), F32)

    def z_unit(zoff, y, c):
        return lax.rem(z + zoff + nz, nz) * 4 + 2 * y + c

    arrived(feats.at[partner], ag_recv.at[partner])
    pass_on(partner, [up, down, sib])

    link_copy.wait()
    tile_copy.wait()

    def forward_steps(first, last_step):
        def one(n, carry):
            u = step_of(n)
            s = lax.rem(b - u + blocks, blocks)
            seen = feats[u]
            both = jnp.concatenate([seen[:tile], seen[tile:]], axis=1)
            for k in range(cap):
                product = jnp.dot(tiles[s * cap + k], both, preferred_element_type=F32)
                use_second = jnp.full((tile, feat), src[s, k], jnp.int32) == 1
                term = jnp.where(use_second, product[:, feat:], product[:, :feat])
                chain[n * cap + k] = term + chain[links[s, k]]
            return carry

        lax.fori_loop(first, last_step, one, 0)

    def own_core_units(d):
        if d < half:
            return [(-d, 0, up), (d, 0, down), (-d, 1, up), (d, 1, down)]
        return [(half, 0, up), (half, 1, down)]

    for d in range(half + 1):
        if d >= 1:
            for zoff, y, target in own_core_units(d):
                u = z_unit(zoff, y, core)
                arrived(feats.at[u], ag_recv.at[u])
                go_on = d + 1 < half or (d + 1 == half and (y == 0) == (zoff < 0))
                pass_on(u, [target, sib] if go_on else [sib])
        if d >= 1:
            wait_d = d - 1
            if wait_d == 0:
                others = [sib, diag]
            else:
                others = [z_unit(zoff, y, 1 - core) for zoff, y, _ in own_core_units(wait_d)]
            for u in others:
                arrived(feats.at[u], ag_recv.at[u])
            if wait_d == 0:
                forward_steps(0, 4)
            else:
                forward_steps(8 * wait_d - 4, 8 * wait_d + 4)
    for zoff, y, _ in own_core_units(half):
        u = z_unit(zoff, y, 1 - core)
        arrived(feats.at[u], ag_recv.at[u])
    forward_steps(8 * half - 4, 8 * half)

    def partial_of(t):
        return chain[links[blocks, t]]

    for i, rep in enumerate(rep_peers):
        for j in range(2):
            part[rep, j * tile:(j + 1) * tile] = partial_of(rep * 2 + j)
        send(part.at[rep], part_in.at[r], rs_send.at[i], rs_recv.at[r], b, rep)
    aggregate = jnp.concatenate([partial_of(r * 2), partial_of(r * 2 + 1)], axis=0)
    for rep in rep_peers:
        arrived(part_in.at[rep], rs_recv.at[rep])
        aggregate = aggregate + part_in[rep]

    pre_act = jnp.dot(aggregate, weight[...], precision=HIGHEST, preferred_element_type=F32) + bias[...]
    sigma = jax.nn.sigmoid(pre_act)
    act_out[...] = pre_act * sigma
    pre_grad = cotangent[...] * sigma * (1.0 + pre_act * (1.0 - sigma))
    agg_grad_t = lax.dot_general(
        weight[...], pre_grad, (((1,), (1,)), ((), ())), precision=HIGHEST, preferred_element_type=F32
    ).astype(BF16)
    for j in range(2):
        grads_t[2 * r + j] = agg_grad_t[:, j * tile:(j + 1) * tile]
    for i, rep in enumerate(rep_peers):
        mine = grads_t.at[pl.ds(2 * r, 2)]
        send(mine, mine, g_send.at[i], g_recv.at[r], b, rep)

    wterm[...] = lax.dot_general(
        aggregate, pre_grad, (((0,), (0,)), ((), ())), precision=HIGHEST, preferred_element_type=F32
    ) * (1.0 / math.sqrt(node_total))
    w_rows = feat // reps
    w_count = [0]

    def w_send_to(src_ref, dst_ref, recv_sem, blk, rep):
        send(src_ref, dst_ref, w_send.at[w_count[0]], recv_sem, blk, rep)
        w_count[0] += 1

    for rep in rep_peers:
        w_send_to(wterm.at[pl.ds(rep * w_rows, w_rows)], wrep.at[r], w1_recv.at[r], b, rep)
    for rep in rep_peers:
        theirs = grads_t.at[pl.ds(2 * rep, 2)]
        arrived(theirs, g_recv.at[rep])

    def w_stage(stage):
        if stage == 0:
            total = wterm[pl.ds(r * w_rows, w_rows)]
            for rep in rep_peers:
                arrived(wrep.at[rep], w1_recv.at[rep])
                total = total + wrep[rep]
            place = lax.rem(b, 4)
            wquad[place] = total
            for blk in [sib, partner, diag]:
                w_send_to(wquad.at[place], wquad.at[place], w2_recv.at[place], blk, r)
        elif stage == 1:
            for blk in [sib, partner, diag]:
                place = lax.rem(blk, 4)
                arrived(wquad.at[place], w2_recv.at[place])
            total = wquad[0]
            for i in range(1, 4):
                total = total + wquad[i]
            wz[z] = total
            for blk in z_peers:
                w_send_to(wz.at[z], wz.at[z], w3_recv.at[z], blk, r)
        elif stage == 2:
            for blk in z_peers:
                arrived(wz.at[blk // 4], w3_recv.at[blk // 4])
            total = wz[0]
            for i in range(1, nz):
                total = total + wz[i]
            wall[r] = total
            for rep in rep_peers:
                w_send_to(wall.at[r], wall.at[r], w4_recv.at[r], b, rep)
        else:
            for rep in rep_peers:
                arrived(wall.at[rep], w4_recv.at[rep])
            wgrad_out[...] = wall[...].reshape(feat, feat)

    def backward_unit(u):
        s = lax.rem(b - u + blocks, blocks)
        first, second = [], []
        for k in range(cap):
            rows = grads_t[dst[s, k]]
            side = jnp.full(rows.shape, jnp.where(k < counts[s], src[s, k], 2), jnp.int32)
            first.append(jnp.where(side == 0, rows, jnp.zeros_like(rows)))
            second.append(jnp.where(side == 1, rows, jnp.zeros_like(rows)))
        picked = jnp.concatenate(
            [jnp.concatenate(first, axis=1), jnp.concatenate(second, axis=1)], axis=0
        )
        stacked = tiles[pl.ds(s * cap, cap)].reshape(cap * tile, tile)
        return jnp.dot(picked, stacked, preferred_element_type=F32)

    index = [0]
    z_count = [0]
    for dist in range(half, -1, -1):
        if dist == half:
            entries = [(half, 0, 0), (half, 1, 1)]
        elif dist >= 1:
            entries = [(dist, 0, 0), (-dist, 0, 1), (dist, 1, 0), (-dist, 1, 1)]
        else:
            entries = [(0, 0, None), (0, 1, None)]
        slots = []
        for zoff, y, way in entries:
            i = index[0]
            index[0] += 1
            slots.append(i)
            sib_out[i] = backward_unit(z_unit(zoff, y, 1 - core))
            send(sib_out.at[i], sib_in.at[i], sib_send.at[i], sib_recv.at[i], sib, r)
        for i, (zoff, y, way) in zip(slots, entries):
            total = backward_unit(z_unit(zoff, y, core))
            arrived(sib_in.at[i], sib_recv.at[i])
            total = total + sib_in[i]
            if dist == 0:
                ways = [0, 1]
            elif dist == half:
                ways = []
            else:
                ways = [way]
            for w in ways:
                if dist == half - 1 and w != y:
                    continue
                arrived(z_in.at[w, dist, y], z_recv.at[w, dist, y])
                total = total + z_in[w, dist, y]
            own_sum[i] = total
            if dist >= 1:
                target = up if way == 0 else down
                send(
                    own_sum.at[i], z_in.at[way, dist - 1, y],
                    z_send.at[z_count[0]], z_recv.at[way, dist - 1, y], target, r,
                )
                z_count[0] += 1
        if half - dist < 4:
            w_stage(half - dist)
    for stage in range(half + 1, 4):
        w_stage(stage)
    base = index[0] - 2
    send(own_sum.at[base + 1 - yh], y_in, y_send, y_recv, partner, r)
    arrived(y_in, y_recv)
    grad_out[...] = own_sum[base + yh] + y_in[...]

    for copy in sent:
        copy.wait_send()


def body(features, adj_tiles, tile_counts, dst_tile, src_tile, weight, bias_term, cotangent):
    blocks = lax.axis_size("blk")
    reps = lax.axis_size("rep")
    steps, cap, tile = adj_tiles.shape[2:5]
    rows, feat = features.shape
    node_total = rows * blocks * reps
    n_slots = steps * cap
    nz = blocks // 4
    half = nz // 2
    w_rows = feat // reps
    dst = dst_tile[0, 0]
    vmem = pl.BlockSpec(memory_space=pltpu.VMEM)
    smem = pl.BlockSpec(memory_space=pltpu.SMEM)
    dma = pltpu.SemaphoreType.DMA
    act, grad_t, wgrad = pl.pallas_call(
        functools.partial(kernel, blocks, reps, node_total),
        out_shape=(
            jax.ShapeDtypeStruct((rows, feat), F32),
            jax.ShapeDtypeStruct((rows, feat), F32),
            jax.ShapeDtypeStruct((feat, feat), F32),
        ),
        in_specs=[vmem, pl.BlockSpec(memory_space=pl.ANY), smem, smem, smem, vmem, vmem, vmem, vmem],
        out_specs=(vmem, vmem, vmem),
        scratch_shapes=[
            pltpu.VMEM((n_slots, tile, tile), BF16),
            pltpu.VMEM((blocks, rows, feat), BF16),
            pltpu.VMEM((n_slots + 1, tile, feat), F32),
            pltpu.VMEM((blocks + 8, 128), jnp.int32),
            pltpu.SMEM((blocks + 8, 128), jnp.int32),
            pltpu.VMEM((reps, rows, feat), F32),
            pltpu.VMEM((reps, rows, feat), F32),
            pltpu.VMEM((2 * reps, feat, tile), BF16),
            pltpu.VMEM((feat, feat), F32),
            pltpu.VMEM((reps, w_rows, feat), F32),
            pltpu.VMEM((4, w_rows, feat), F32),
            pltpu.VMEM((nz, w_rows, feat), F32),
            pltpu.VMEM((reps, w_rows, feat), F32),
            pltpu.VMEM((blocks // 2, 2 * feat, tile), F32),
            pltpu.VMEM((blocks // 2, 2 * feat, tile), F32),
            pltpu.VMEM((blocks // 2, 2 * feat, tile), F32),
            pltpu.VMEM((2, half, 2, 2 * feat, tile), F32),
            pltpu.VMEM((2 * feat, tile), F32),
            dma, dma,
            dma((blocks,)), dma((blocks,)),
            dma((reps,)), dma((reps,)),
            dma((reps,)), dma((reps,)),
            dma((2 * reps + nz + 4,)), dma((reps,)), dma((4,)), dma((nz,)), dma((reps,)),
            dma((blocks // 2,)), dma((blocks // 2,)),
            dma((2 * nz,)), dma((2, half, 2)),
            dma, dma,
        ],
        compiler_params=pltpu.CompilerParams(
            collective_id=0, has_side_effects=True, vmem_limit_bytes=58 * 1024 * 1024
        ),
        cost_estimate=pl.CostEstimate(
            flops=4 * n_slots * tile * tile * feat,
            bytes_accessed=n_slots * tile * tile * 2,
            transcendentals=rows * feat,
        ),
        name="graph_layer",
    )(
        features, adj_tiles.reshape(n_slots, tile, tile), tile_counts[0, 0], dst, src_tile[0, 0],
        dst, weight, bias_term.reshape(1, feat), cotangent,
    )
    feature_grad = jnp.swapaxes(grad_t.reshape(2, feat, tile), 1, 2).reshape(rows, feat)
    return act, feature_grad, wgrad


def solution(mesh):
    in_specs = (
        P(("blk", "rep"), None),
        P("blk", "rep", None, None, None, None),
        P("blk", "rep", None),
        P("blk", "rep", None, None),
        P("blk", "rep", None, None),
        P(),
        P(),
        P(("blk", "rep"), None),
    )
    out_specs = (P(("blk", "rep"), None), P(("blk", "rep"), None), P())
    return jax.shard_map(body, mesh=mesh, in_specs=in_specs, out_specs=out_specs, check_vma=False)
```

```python
import functools
import math

import jax
import jax.numpy as jnp
from jax import lax
from jax.experimental import pallas as pl
from jax.experimental.pallas import tpu as pltpu
from jax.sharding import PartitionSpec as P

MESH = pl.DeviceIdType.MESH
F32 = jnp.float32
BF16 = jnp.bfloat16
HIGHEST = lax.Precision.HIGHEST
I16 = jnp.int16
SCALE_ROWS = 16
PIECES = 2


def encode(ref, value):
    rows = value.shape[0]
    largest = jnp.max(jnp.abs(value), axis=0, keepdims=True)
    power = jnp.clip(jnp.floor(14.9 - jnp.log2(largest)), -120.0, 120.0)
    ref[0:rows] = jnp.round(value * jnp.exp2(power)).astype(jnp.int32).astype(I16)
    ref[rows:rows + SCALE_ROWS] = jnp.broadcast_to(
        power.astype(jnp.int32), (SCALE_ROWS, value.shape[1])
    ).astype(I16)


def decode(ref):
    rows = ref.shape[0] - SCALE_ROWS
    scale = jnp.exp2(-ref[rows:rows + SCALE_ROWS].astype(jnp.int32).astype(F32))
    value = ref[0:rows].astype(jnp.int32).astype(F32)
    grouped = value.reshape(rows // SCALE_ROWS, SCALE_ROWS, value.shape[1]) * scale[None]
    return grouped.reshape(value.shape)


def kernel(
    blocks, reps, node_total,
    features, tiles_hbm, counts_hbm, dst_hbm, src_hbm, weight_hbm, bias_hbm, cotangent_hbm,
    act_out, grad_out, wgrad_out,
    counts, dst, src, dst_vec, weight, bias, cotangent, tiles, feats, chain, links_vec, links,
    part, part_in, grads_t, wterm, wrep, wquad, wz, wall,
    sib_out, sib_in, own_sum, z_out, z_in, y_in,
    in_sems, tile_sem, link_sem, ag_send, ag_recv, rs_send, rs_recv, g_send, g_recv,
    w_send, w1_recv, w2_recv, w3_recv, w4_recv,
    sib_send, sib_recv, z_send, z_recv, y_recv,
):
    nz = blocks // 4
    half = nz // 2
    cap = dst.shape[0]
    tile = tiles.shape[1]
    feat = features.shape[1]
    n_slots = blocks * cap
    b = lax.axis_index("blk")
    r = lax.axis_index("rep")
    core = lax.rem(b, 2)
    yh = lax.rem(b // 2, 2)
    z = b // 4
    sib = b + 1 - 2 * core
    partner = b + 2 - 4 * yh
    diag = sib + 2 - 4 * yh
    up = lax.rem(b + 4, blocks)
    down = lax.rem(b + blocks - 4, blocks)

    sent = []

    def send(src_ref, dst_ref, send_sem, recv_sem, blk, rep):
        copy = pltpu.make_async_remote_copy(
            src_ref=src_ref, dst_ref=dst_ref, send_sem=send_sem, recv_sem=recv_sem,
            device_id=(blk, rep), device_id_type=MESH,
        )
        copy.start()
        sent.append(copy)

    def arrived(dst_ref, recv_sem):
        pltpu.make_async_remote_copy(
            src_ref=dst_ref, dst_ref=dst_ref, send_sem=w_send.at[0], recv_sem=recv_sem,
            device_id=(sib, r), device_id_type=MESH,
        ).wait_recv()

    z_peers = [lax.rem(b + 4 * i, blocks) for i in range(1, nz)]
    rep_peers = [lax.rem(r + i, reps) for i in range(1, reps)]
    partner_up = lax.rem(partner + 4, blocks)
    partner_down = lax.rem(partner + blocks - 4, blocks)
    blk_peers = [sib, partner, diag, partner_up, partner_down] + z_peers
    barrier = pltpu.get_barrier_semaphore()
    for blk in blk_peers:
        pl.semaphore_signal(barrier, inc=1, device_id=(blk, r), device_id_type=MESH)
    for rep in rep_peers:
        pl.semaphore_signal(barrier, inc=1, device_id=(b, rep), device_id_type=MESH)
    copies = [
        pltpu.make_async_copy(from_ref, to_ref, in_sems.at[i])
        for i, (from_ref, to_ref) in enumerate([
            (features, feats.at[b]), (dst_hbm, dst_vec), (dst_hbm, dst), (counts_hbm, counts),
            (src_hbm, src), (weight_hbm, weight), (bias_hbm, bias), (cotangent_hbm, cotangent),
        ])
    ]
    own_copy, index_copies, dense_copies = copies[0], copies[1:5], copies[5:]
    own_copy.start()
    for copy in index_copies:
        copy.start()
    tile_copy = pltpu.make_async_copy(tiles_hbm, tiles, tile_sem)
    tile_copy.start()
    for copy in dense_copies:
        copy.start()
    pl.semaphore_wait(barrier, len(blk_peers) + len(rep_peers))

    ag_count = [0]
    piece = features.shape[0] // PIECES

    def pass_on(u, target, first, n_rows, flag):
        rows = feats.at[u, pl.ds(first, n_rows)]
        send(rows, rows, ag_send.at[ag_count[0]], ag_recv.at[u, flag], target, r)
        ag_count[0] += 1

    def to_sibling(u):
        pass_on(u, sib, 0, PIECES * piece, 0)

    def unit_arrived(u):
        arrived(feats.at[u], ag_recv.at[u, 0])

    own_copy.wait()
    for targets in ((up, down), (partner_up, partner_down, partner)):
        for h in range(PIECES):
            for target in targets:
                pass_on(b, target, h * piece, piece, h)
    to_sibling(b)
    for copy in index_copies:
        copy.wait()

    groups = [("own", 0)]
    for d in range(1, half + 1):
        groups += [("own", d), ("other", d)]
        if d == 1:
            groups.append(("other", 0))

    def group_size(group):
        return 2 if group[1] in (0, half) else 4

    starts = {}
    total_steps = 0
    for group in groups:
        starts[group] = total_steps
        total_steps += group_size(group)

    def unit_in(group, j):
        which, d = group
        y = yh if which == "own" else 1 - yh
        if group_size(group) == 2:
            zoff, c = d, j
        else:
            zoff, c = nz + d * (2 * lax.rem(j, 2) - 1), j // 2
        return lax.rem(z + zoff, nz) * 4 + 2 * y + lax.rem(core + c, 2)

    dst_tab = dst_vec[...]
    slot_iota = lax.broadcasted_iota(jnp.int32, dst_tab.shape, 1) * cap + lax.broadcasted_iota(
        jnp.int32, dst_tab.shape, 0
    )
    tile_iota = lax.broadcasted_iota(jnp.int32, (8, 128), 1)

    def link_step(group, j, carry):
        current, before, last = carry
        n = starts[group] + j
        s = lax.rem(b - unit_in(group, j) + blocks, blocks)
        for k in range(cap):
            to = jnp.where(k < counts[s], dst[k, s], -1)
            before = jnp.where(slot_iota == s * cap + k, current, before)
            current = jnp.where(dst_tab == to, n * cap + k, current)
            last = jnp.where(tile_iota == to, n * cap + k, last)
        return current, before, last

    nothing = jnp.full(dst_tab.shape, n_slots, jnp.int32)
    carry = (nothing, nothing, jnp.full((8, 128), n_slots, jnp.int32))
    for group in groups:
        carry = lax.fori_loop(0, group_size(group), functools.partial(link_step, group), carry)
    _, before, last = carry
    links_vec[...] = jnp.zeros(links_vec.shape, jnp.int32)
    links_vec[0:cap, 0:blocks] = before
    links_vec[8:16, :] = last
    link_copy = pltpu.make_async_copy(links_vec, links, link_sem)
    link_copy.start()
    chain[n_slots] = jnp.zeros((tile, feat), F32)

    def z_unit(zoff, y, c):
        return lax.rem(z + zoff + nz, nz) * 4 + 2 * y + c

    def z_unit(zoff, y, c):
        return lax.rem(z + zoff + nz, nz) * 4 + 2 * y + c

    def take_in(group):
        which, d = group
        y = yh if which == "own" else 1 - yh
        if d in (0, half):
            moves = [(d, None)]
        else:
            moves = [
                (zoff, target if d + 1 < half or which == last_y else None)
                for zoff, target, last_y in ((-d, up, "own"), (d, down, "other"))
            ]
        for h in range(PIECES):
            for zoff, target in moves:
                u = z_unit(zoff, y, core)
                arrived(feats.at[u, pl.ds(h * piece, piece)], ag_recv.at[u, h])
                if target is not None:
                    pass_on(u, target, h * piece, piece, h)
        for zoff, _ in moves:
            to_sibling(z_unit(zoff, y, core))

    def work_on(group):
        which, d = group
        y = yh if which == "own" else 1 - yh
        for zoff in (d,) if d in (0, half) else (-d, d):
            unit_arrived(z_unit(zoff, y, 1 - core))

        def one(j, carry):
            u = unit_in(group, j)
            n = starts[group] + j
            s = lax.rem(b - u + blocks, blocks)
            seen = feats[u]
            both = jnp.concatenate([seen[:tile], seen[tile:]], axis=1)
            for k in range(cap):
                product = jnp.dot(tiles[s * cap + k], both, preferred_element_type=F32)
                use_second = jnp.full((tile, feat), src[k, s], jnp.int32) == 1
                term = jnp.where(use_second, product[:, feat:], product[:, :feat])
                chain[n * cap + k] = term + chain[links[k, s]]
            return carry

        lax.fori_loop(0, group_size(group), one, 0)

    for i, group in enumerate(groups):
        if i == len(groups) - 1:
            work_on(groups[i - 2])
        if i >= 1:
            take_in(group)
        if i == 1:
            link_copy.wait()
            tile_copy.wait()
        if 2 <= i < len(groups) - 1:
            work_on(groups[i - 2])
    work_on(groups[-2])
    work_on(groups[-1])

    def partial_of(t):
        return chain[links[8, t]]

    for i, rep in enumerate(rep_peers):
        encode(part.at[rep], jnp.concatenate([partial_of(rep * 2), partial_of(rep * 2 + 1)], axis=0))
        send(part.at[rep], part_in.at[r], rs_send.at[i], rs_recv.at[r], b, rep)
    aggregate = jnp.concatenate([partial_of(r * 2), partial_of(r * 2 + 1)], axis=0)
    for copy in dense_copies:
        copy.wait()
    for rep in rep_peers:
        arrived(part_in.at[rep], rs_recv.at[rep])
        aggregate = aggregate + decode(part_in.at[rep])

    pre_act = jnp.dot(aggregate, weight[...], precision=HIGHEST, preferred_element_type=F32) + bias[...]
    sigma = jax.nn.sigmoid(pre_act)
    pre_grad = cotangent[...] * sigma * (1.0 + pre_act * (1.0 - sigma))
    agg_grad_t = lax.dot_general(
        weight[...], pre_grad, (((1,), (1,)), ((), ())), precision=HIGHEST, preferred_element_type=F32
    ).astype(BF16)
    for j in range(2):
        grads_t[2 * r + j] = agg_grad_t[:, j * tile:(j + 1) * tile]
    for i, rep in enumerate(rep_peers):
        mine = grads_t.at[pl.ds(2 * r, 2)]
        send(mine, mine, g_send.at[i], g_recv.at[r], b, rep)

    act_out[...] = pre_act * sigma

    wterm[...] = lax.dot_general(
        aggregate, pre_grad, (((0,), (0,)), ((), ())), precision=HIGHEST, preferred_element_type=F32
    ) * (1.0 / math.sqrt(node_total))
    w_rows = feat // reps
    w_count = [0]

    def w_send_to(src_ref, dst_ref, recv_sem, blk, rep):
        send(src_ref, dst_ref, w_send.at[w_count[0]], recv_sem, blk, rep)
        w_count[0] += 1

    for rep in rep_peers:
        w_send_to(wterm.at[pl.ds(rep * w_rows, w_rows)], wrep.at[r], w1_recv.at[r], b, rep)
    for rep in rep_peers:
        theirs = grads_t.at[pl.ds(2 * rep, 2)]
        arrived(theirs, g_recv.at[rep])

    w_done = [0]

    def w_stage(stage):
        w_done[0] += 1
        if stage == 0:
            total = wterm[pl.ds(r * w_rows, w_rows)]
            for rep in rep_peers:
                arrived(wrep.at[rep], w1_recv.at[rep])
                total = total + wrep[rep]
            place = lax.rem(b, 4)
            wquad[place] = total
            for blk in [sib, partner, diag]:
                w_send_to(wquad.at[place], wquad.at[place], w2_recv.at[place], blk, r)
        elif stage == 1:
            for blk in [sib, partner, diag]:
                place = lax.rem(blk, 4)
                arrived(wquad.at[place], w2_recv.at[place])
            total = wquad[0]
            for i in range(1, 4):
                total = total + wquad[i]
            wz[z] = total
            for blk in z_peers:
                w_send_to(wz.at[z], wz.at[z], w3_recv.at[z], blk, r)
        elif stage == 2:
            for blk in z_peers:
                arrived(wz.at[blk // 4], w3_recv.at[blk // 4])
            total = wz[0]
            for i in range(1, nz):
                total = total + wz[i]
            wall[r] = total
            for rep in rep_peers:
                w_send_to(wall.at[r], wall.at[r], w4_recv.at[r], b, rep)
        else:
            for rep in rep_peers:
                arrived(wall.at[rep], w4_recv.at[rep])
            wgrad_out[...] = wall[...].reshape(feat, feat)

    def backward_unit(u):
        s = lax.rem(b - u + blocks, blocks)
        first, second = [], []
        for k in range(cap):
            rows = grads_t[dst[k, s]]
            side = jnp.full(rows.shape, jnp.where(k < counts[s], src[k, s], 2), jnp.int32)
            first.append(jnp.where(side == 0, rows, jnp.zeros_like(rows)))
            second.append(jnp.where(side == 1, rows, jnp.zeros_like(rows)))
        picked = jnp.concatenate(
            [jnp.concatenate(first, axis=1), jnp.concatenate(second, axis=1)], axis=0
        )
        stacked = tiles[pl.ds(s * cap, cap)].reshape(cap * tile, tile)
        return jnp.dot(picked, stacked, preferred_element_type=F32)

    index = 0
    for dist in range(half, -1, -1):
        if dist == half:
            entries = [(half, 0, [], 0), (half, 1, [], 1)]
            if half > 1:
                entries += [(half - 1, 1, [], 0), (1 - half, 0, [], 1)]
        elif dist == half - 1 and dist >= 1:
            entries = [(dist, 0, [0], 0), (-dist, 1, [1], 1)]
        elif dist >= 1:
            entries = [
                (zoff, y, [way], way) for y in range(2) for way, zoff in enumerate((dist, -dist))
            ]
        else:
            entries = [(0, 1, [0, 1] if half > 1 else [1], None)]
        if dist == min(2, half):
            entries.append((0, 0, [], None))
        units = [(index + i, zoff, (yh + 1 - y) % 2) for i, (zoff, y, _, _) in enumerate(entries)]
        index += len(entries)
        for i, zoff, y in units:
            encode(sib_out.at[i], backward_unit(z_unit(zoff, y, 1 - core)))
            send(sib_out.at[i], sib_in.at[i], sib_send.at[i], sib_recv.at[i], sib, r)
        for i, zoff, y in units:
            own_sum[i] = backward_unit(z_unit(zoff, y, core))
        if dist < half - 1 and w_done[0] < 3:
            w_stage(w_done[0])
        for i, _, _ in units:
            arrived(sib_in.at[i], sib_recv.at[i])
            own_sum[i] = own_sum[i] + decode(sib_in.at[i])
        for (i, _, _), (zoff, y, ways, way) in zip(units, entries):
            for j in range(2):
                value = own_sum[i, j * feat:(j + 1) * feat]
                for w in ways:
                    arrived(z_in.at[w, abs(zoff), y, j], z_recv.at[w, abs(zoff), y, j])
                    value = value + decode(z_in.at[w, abs(zoff), y, j])
                if zoff == 0 and y == 1:
                    for k in range(3):
                        arrived(y_in.at[k, j], y_recv.at[k, j])
                        value = value + decode(y_in.at[k, j])
                    grad_out[j * feat:(j + 1) * feat] = value
                    continue
                out = z_out.at[i, j]
                encode(out, value)
                if zoff == 0:
                    target, place, flag = partner, y_in.at[2, j], y_recv.at[2, j]
                elif abs(zoff) == 1 and y == 0:
                    target = partner_up if way == 0 else partner_down
                    place, flag = y_in.at[way, j], y_recv.at[way, j]
                else:
                    target = up if way == 0 else down
                    near = abs(zoff) - 1
                    place, flag = z_in.at[way, near, y, j], z_recv.at[way, near, y, j]
                send(out, place, z_send.at[i, j], flag, target, r)
        if dist == half:
            w_stage(0)
    for stage in range(w_done[0], 4):
        w_stage(stage)

    for copy in sent:
        copy.wait_send()


def finish(act, grad_t, wgrad, act_out, grad_out, wgrad_out):
    act_out[...] = act[...]
    wgrad_out[...] = wgrad[...]
    feat = wgrad.shape[0]
    tile = grad_t.shape[1]
    for j in range(2):
        grad_out[j * tile:(j + 1) * tile] = grad_t[j * feat:(j + 1) * feat].T


def body(features, adj_tiles, tile_counts, dst_tile, src_tile, weight, bias_term, cotangent):
    blocks = lax.axis_size("blk")
    reps = lax.axis_size("rep")
    steps, cap, tile = adj_tiles.shape[2:5]
    rows, feat = features.shape
    node_total = rows * blocks * reps
    n_slots = steps * cap
    nz = blocks // 4
    half = nz // 2
    w_rows = feat // reps
    dst = dst_tile[0, 0].T
    src = src_tile[0, 0].T
    shapes = (
        jax.ShapeDtypeStruct((rows, feat), F32),
        jax.ShapeDtypeStruct((rows, feat), F32),
        jax.ShapeDtypeStruct((feat, feat), F32),
    )
    vmem = pl.BlockSpec(memory_space=pltpu.VMEM)
    dma = pltpu.SemaphoreType.DMA
    act, grad_t, wgrad = pl.pallas_call(
        functools.partial(kernel, blocks, reps, node_total),
        out_shape=shapes,
        in_specs=[pl.BlockSpec(memory_space=pltpu.HBM)] * 8,
        out_specs=(vmem, vmem, vmem),
        scratch_shapes=[
            pltpu.SMEM((blocks,), jnp.int32),
            pltpu.SMEM((cap, blocks), jnp.int32),
            pltpu.SMEM((cap, blocks), jnp.int32),
            pltpu.VMEM((cap, blocks), jnp.int32),
            pltpu.VMEM((feat, feat), F32),
            pltpu.VMEM((1, feat), F32),
            pltpu.VMEM((rows, feat), F32),
            pltpu.VMEM((n_slots, tile, tile), BF16),
            pltpu.VMEM((blocks, rows, feat), BF16),
            pltpu.VMEM((n_slots + 1, tile, feat), F32),
            pltpu.VMEM((16, 128), jnp.int32),
            pltpu.SMEM((16, 128), jnp.int32),
            pltpu.VMEM((reps, rows + SCALE_ROWS, feat), I16),
            pltpu.VMEM((reps, rows + SCALE_ROWS, feat), I16),
            pltpu.VMEM((2 * reps, feat, tile), BF16),
            pltpu.VMEM((feat, feat), F32),
            pltpu.VMEM((reps, w_rows, feat), F32),
            pltpu.VMEM((4, w_rows, feat), F32),
            pltpu.VMEM((nz, w_rows, feat), F32),
            pltpu.VMEM((reps, w_rows, feat), F32),
            pltpu.VMEM((blocks // 2, 2 * feat + SCALE_ROWS, tile), I16),
            pltpu.VMEM((blocks // 2, 2 * feat + SCALE_ROWS, tile), I16),
            pltpu.VMEM((blocks // 2, 2 * feat, tile), F32),
            pltpu.VMEM((blocks // 2, 2, feat + SCALE_ROWS, tile), I16),
            pltpu.VMEM((2, half, 2, 2, feat + SCALE_ROWS, tile), I16),
            pltpu.VMEM((3, 2, feat + SCALE_ROWS, tile), I16),
            dma((8,)), dma, dma,
            dma((PIECES * 2 * blocks,)), dma((blocks, PIECES)),
            dma((reps,)), dma((reps,)),
            dma((reps,)), dma((reps,)),
            dma((2 * reps + nz + 4,)), dma((reps,)), dma((4,)), dma((nz,)), dma((reps,)),
            dma((blocks // 2,)), dma((blocks // 2,)),
            dma((blocks // 2, 2)), dma((2, half, 2, 2)),
            dma((3, 2)),
        ],
        compiler_params=pltpu.CompilerParams(
            collective_id=0, has_side_effects=True, vmem_limit_bytes=58 * 1024 * 1024
        ),
        cost_estimate=pl.CostEstimate(
            flops=4 * n_slots * tile * tile * feat,
            bytes_accessed=n_slots * tile * tile * 2,
            transcendentals=rows * feat,
        ),
        name="graph_layer",
    )(
        features, adj_tiles.reshape(n_slots, tile, tile), tile_counts[0, 0], dst, src,
        weight, bias_term.reshape(1, feat), cotangent,
    )
    return pl.pallas_call(finish, out_shape=shapes, name="outputs")(act, grad_t, wgrad)


def solution(mesh):
    in_specs = (
        P(("blk", "rep"), None),
        P("blk", "rep", None, None, None, None),
        P("blk", "rep", None),
        P("blk", "rep", None, None),
        P("blk", "rep", None, None),
        P(),
        P(),
        P(("blk", "rep"), None),
    )
    out_specs = (P(("blk", "rep"), None), P(("blk", "rep"), None), P())
    return jax.shard_map(body, mesh=mesh, in_specs=in_specs, out_specs=out_specs, check_vma=False)
```

```python
import functools
import math

import jax
import jax.numpy as jnp
from jax import lax
from jax.experimental import pallas as pl
from jax.experimental.pallas import tpu as pltpu
from jax.sharding import PartitionSpec as P

MESH = pl.DeviceIdType.MESH
F32 = jnp.float32
BF16 = jnp.bfloat16
HIGHEST = lax.Precision.HIGHEST
I16 = jnp.int16
SCALE_ROWS = 16
PIECES = 1


def encode(ref, value):
    rows = value.shape[0]
    largest = jnp.max(jnp.abs(value), axis=0, keepdims=True)
    power = jnp.clip(jnp.floor(14.9 - jnp.log2(largest)), -120.0, 120.0)
    ref[0:rows] = jnp.round(value * jnp.exp2(power)).astype(jnp.int32).astype(I16)
    ref[rows:rows + SCALE_ROWS] = jnp.broadcast_to(
        power.astype(jnp.int32), (SCALE_ROWS, value.shape[1])
    ).astype(I16)


def decode(ref):
    rows = ref.shape[0] - SCALE_ROWS
    scale = jnp.exp2(-ref[rows:rows + SCALE_ROWS].astype(jnp.int32).astype(F32))
    value = ref[0:rows].astype(jnp.int32).astype(F32)
    grouped = value.reshape(rows // SCALE_ROWS, SCALE_ROWS, value.shape[1]) * scale[None]
    return grouped.reshape(value.shape)


def kernel(
    blocks, reps, node_total,
    features, tiles_hbm, counts_hbm, dst_hbm, src_hbm, weight_hbm, bias_hbm, cotangent_hbm,
    act_out, grad_out, wgrad_out,
    counts, dst, src, dst_vec, weight, bias, cotangent, tiles, feats, chain, links_vec, links,
    part, part_in, grads_t, wterm, wrep, wquad, wz, wall,
    sib_out, sib_in, own_sum, z_out, z_in, y_in,
    in_sems, tile_sem, link_sem, ag_send, ag_recv, rs_send, rs_recv, g_send, g_recv,
    w_send, w1_recv, w2_recv, w3_recv, w4_recv,
    sib_send, sib_recv, z_send, z_recv, y_recv,
):
    nz = blocks // 4
    half = nz // 2
    cap = dst.shape[0]
    tile = tiles.shape[1]
    feat = features.shape[1]
    n_slots = blocks * cap
    b = lax.axis_index("blk")
    r = lax.axis_index("rep")
    core = lax.rem(b, 2)
    yh = lax.rem(b // 2, 2)
    z = b // 4
    sib = b + 1 - 2 * core
    partner = b + 2 - 4 * yh
    diag = sib + 2 - 4 * yh
    up = lax.rem(b + 4, blocks)
    down = lax.rem(b + blocks - 4, blocks)

    sent = []

    def send(src_ref, dst_ref, send_sem, recv_sem, blk, rep):
        copy = pltpu.make_async_remote_copy(
            src_ref=src_ref, dst_ref=dst_ref, send_sem=send_sem, recv_sem=recv_sem,
            device_id=(blk, rep), device_id_type=MESH,
        )
        copy.start()
        sent.append(copy)

    def settle(keep=0):
        while len(sent) > keep:
            sent.pop(0).wait_send()

    def arrived(dst_ref, recv_sem):
        pltpu.make_async_remote_copy(
            src_ref=dst_ref, dst_ref=dst_ref, send_sem=w_send.at[0], recv_sem=recv_sem,
            device_id=(sib, r), device_id_type=MESH,
        ).wait_recv()

    z_peers = [lax.rem(b + 4 * i, blocks) for i in range(1, nz)]
    rep_peers = [lax.rem(r + i, reps) for i in range(1, reps)]
    partner_up = lax.rem(partner + 4, blocks)
    partner_down = lax.rem(partner + blocks - 4, blocks)
    blk_peers = [sib, partner, diag, partner_up, partner_down] + z_peers
    barrier = pltpu.get_barrier_semaphore()
    for blk in blk_peers:
        pl.semaphore_signal(barrier, inc=1, device_id=(blk, r), device_id_type=MESH)
    for rep in rep_peers:
        pl.semaphore_signal(barrier, inc=1, device_id=(b, rep), device_id_type=MESH)
    copies = [
        pltpu.make_async_copy(from_ref, to_ref, in_sems.at[i])
        for i, (from_ref, to_ref) in enumerate([
            (features, feats.at[b]), (dst_hbm, dst_vec), (dst_hbm, dst), (counts_hbm, counts),
            (src_hbm, src), (weight_hbm, weight), (bias_hbm, bias), (cotangent_hbm, cotangent),
        ])
    ]
    own_copy, index_copies, dense_copies = copies[0], copies[1:5], copies[5:]
    own_copy.start()
    for copy in index_copies:
        copy.start()
    tile_copy = pltpu.make_async_copy(tiles_hbm, tiles, tile_sem)
    tile_copy.start()
    for copy in dense_copies:
        copy.start()
    pl.semaphore_wait(barrier, len(blk_peers) + len(rep_peers))

    ag_count = [0]
    piece = features.shape[0] // PIECES

    def pass_on(u, target, first, n_rows, flag):
        rows = feats.at[u, pl.ds(first, n_rows)]
        send(rows, rows, ag_send.at[ag_count[0]], ag_recv.at[u, flag], target, r)
        ag_count[0] += 1

    def to_sibling(u):
        pass_on(u, sib, 0, PIECES * piece, 0)

    def unit_arrived(u):
        arrived(feats.at[u], ag_recv.at[u, 0])

    own_copy.wait()
    for targets in ((up, down), (partner_up, partner_down, partner)):
        for h in range(PIECES):
            for target in targets:
                pass_on(b, target, h * piece, piece, h)
    to_sibling(b)
    for copy in index_copies:
        copy.wait()

    groups = [("own", 0)]
    for d in range(1, half + 1):
        groups += [("own", d), ("other", d)]
        if d == 1:
            groups.append(("other", 0))

    def group_size(group):
        return 2 if group[1] in (0, half) else 4

    starts = {}
    total_steps = 0
    for group in groups:
        starts[group] = total_steps
        total_steps += group_size(group)

    def unit_in(group, j):
        which, d = group
        y = yh if which == "own" else 1 - yh
        if group_size(group) == 2:
            zoff, c = d, j
        else:
            zoff, c = nz + d * (2 * lax.rem(j, 2) - 1), j // 2
        return lax.rem(z + zoff, nz) * 4 + 2 * y + lax.rem(core + c, 2)

    dst_tab = dst_vec[...]
    slot_iota = lax.broadcasted_iota(jnp.int32, dst_tab.shape, 1) * cap + lax.broadcasted_iota(
        jnp.int32, dst_tab.shape, 0
    )
    tile_iota = lax.broadcasted_iota(jnp.int32, (8, 128), 1)

    def link_step(group, j, carry):
        current, before, last = carry
        n = starts[group] + j
        s = lax.rem(b - unit_in(group, j) + blocks, blocks)
        for k in range(cap):
            to = jnp.where(k < counts[s], dst[k, s], -1)
            before = jnp.where(slot_iota == s * cap + k, current, before)
            current = jnp.where(dst_tab == to, n * cap + k, current)
            last = jnp.where(tile_iota == to, n * cap + k, last)
        return current, before, last

    nothing = jnp.full(dst_tab.shape, n_slots, jnp.int32)
    carry = (nothing, nothing, jnp.full((8, 128), n_slots, jnp.int32))
    for group in groups:
        carry = lax.fori_loop(0, group_size(group), functools.partial(link_step, group), carry)
    _, before, last = carry
    links_vec[...] = jnp.zeros(links_vec.shape, jnp.int32)
    links_vec[0:cap, 0:blocks] = before
    links_vec[8:16, :] = last
    link_copy = pltpu.make_async_copy(links_vec, links, link_sem)
    link_copy.start()
    chain[n_slots] = jnp.zeros((tile, feat), F32)

    other_y = 1 - yh
    z_base = {zoff: lax.rem(z + zoff + nz, nz) * 4 for zoff in range(1 - half, half + 1)}

    def z_unit(zoff, y, c):
        return z_base[zoff] + 2 * y + c

    def take_in(group):
        which, d = group
        y = yh if which == "own" else other_y
        if d in (0, half):
            moves = [(d, None)]
        else:
            moves = [
                (zoff, target if d + 1 < half or which == last_y else None)
                for zoff, target, last_y in ((-d, up, "own"), (d, down, "other"))
            ]
        for h in range(PIECES):
            for zoff, target in moves:
                u = z_unit(zoff, y, core)
                arrived(feats.at[u, pl.ds(h * piece, piece)], ag_recv.at[u, h])
                if target is not None:
                    pass_on(u, target, h * piece, piece, h)
        for zoff, _ in moves:
            to_sibling(z_unit(zoff, y, core))

    def work_on(group):
        which, d = group
        y = yh if which == "own" else other_y
        for zoff in (d,) if d in (0, half) else (-d, d):
            unit_arrived(z_unit(zoff, y, 1 - core))

        def one(j, carry):
            u = unit_in(group, j)
            n = starts[group] + j
            s = lax.rem(b - u + blocks, blocks)
            seen = feats[u]
            both = jnp.concatenate([seen[:tile], seen[tile:]], axis=1)
            for k in range(cap):
                product = jnp.dot(tiles[s * cap + k], both, preferred_element_type=F32)
                use_second = jnp.full((tile, feat), src[k, s], jnp.int32) == 1
                term = jnp.where(use_second, product[:, feat:], product[:, :feat])
                chain[n * cap + k] = term + chain[links[k, s]]
            return carry

        lax.fori_loop(0, group_size(group), one, 0)

    for i, group in enumerate(groups):
        if i == len(groups) - 1:
            work_on(groups[i - 2])
        if i >= 1:
            take_in(group)
        if i == 1:
            link_copy.wait()
            tile_copy.wait()
        if 2 <= i < len(groups) - 1:
            work_on(groups[i - 2])
    work_on(groups[-2])
    work_on(groups[-1])

    def partial_of(t):
        return chain[links[8, t]]

    for j in range(2):
        for i, rep in enumerate(rep_peers):
            encode(part.at[rep, j], partial_of(rep * 2 + j))
            send(part.at[rep, j], part_in.at[r, j], rs_send.at[i, j], rs_recv.at[r, j], b, rep)
    settle(2 * len(rep_peers))
    for copy in dense_copies:
        copy.wait()
    terms = []
    for j in range(2):
        aggregate = partial_of(r * 2 + j)
        for rep in rep_peers:
            arrived(part_in.at[rep, j], rs_recv.at[rep, j])
            aggregate = aggregate + decode(part_in.at[rep, j])
        rows = slice(j * tile, (j + 1) * tile)
        pre_act = jnp.dot(
            aggregate, weight[...], precision=HIGHEST, preferred_element_type=F32
        ) + bias[...]
        sigma = jax.nn.sigmoid(pre_act)
        pre_grad = cotangent[rows] * sigma * (1.0 + pre_act * (1.0 - sigma))
        grads_t[2 * r + j] = lax.dot_general(
            weight[...], pre_grad, (((1,), (1,)), ((), ())),
            precision=HIGHEST, preferred_element_type=F32,
        ).astype(BF16)
        mine = grads_t.at[2 * r + j]
        for i, rep in enumerate(rep_peers):
            send(mine, mine, g_send.at[i, j], g_recv.at[r, j], b, rep)
        act_out[rows] = pre_act * sigma
        terms.append((aggregate, pre_grad))

    wterm[...] = sum(
        lax.dot_general(
            aggregate, pre_grad, (((0,), (0,)), ((), ())), precision=HIGHEST, preferred_element_type=F32
        )
        for aggregate, pre_grad in terms
    ) * (1.0 / math.sqrt(node_total))
    w_rows = feat // reps
    w_count = [0]

    def w_send_to(src_ref, dst_ref, recv_sem, blk, rep):
        send(src_ref, dst_ref, w_send.at[w_count[0]], recv_sem, blk, rep)
        w_count[0] += 1

    for rep in rep_peers:
        w_send_to(wterm.at[pl.ds(rep * w_rows, w_rows)], wrep.at[r], w1_recv.at[r], b, rep)
    settle(3 * len(rep_peers))
    for rep in rep_peers:
        for j in range(2):
            arrived(grads_t.at[2 * rep + j], g_recv.at[rep, j])

    w_done = [0]

    def w_stage(stage):
        w_done[0] += 1
        if stage == 0:
            total = wterm[pl.ds(r * w_rows, w_rows)]
            for rep in rep_peers:
                arrived(wrep.at[rep], w1_recv.at[rep])
                total = total + wrep[rep]
            place = lax.rem(b, 4)
            wquad[place] = total
            for blk in [sib, partner, diag]:
                w_send_to(wquad.at[place], wquad.at[place], w2_recv.at[place], blk, r)
        elif stage == 1:
            for blk in [sib, partner, diag]:
                place = lax.rem(blk, 4)
                arrived(wquad.at[place], w2_recv.at[place])
            total = wquad[0]
            for i in range(1, 4):
                total = total + wquad[i]
            wz[z] = total
            for blk in z_peers:
                w_send_to(wz.at[z], wz.at[z], w3_recv.at[z], blk, r)
        elif stage == 2:
            for blk in z_peers:
                arrived(wz.at[blk // 4], w3_recv.at[blk // 4])
            total = wz[0]
            for i in range(1, nz):
                total = total + wz[i]
            wall[r] = total
            for rep in rep_peers:
                w_send_to(wall.at[r], wall.at[r], w4_recv.at[r], b, rep)
        else:
            for rep in rep_peers:
                arrived(wall.at[rep], w4_recv.at[rep])
            wgrad_out[...] = wall[...].reshape(feat, feat)

    def backward_unit(u):
        s = lax.rem(b - u + blocks, blocks)
        first, second = [], []
        for k in range(cap):
            rows = grads_t[dst[k, s]]
            side = jnp.full(rows.shape, jnp.where(k < counts[s], src[k, s], 2), jnp.int32)
            first.append(jnp.where(side == 0, rows, jnp.zeros_like(rows)))
            second.append(jnp.where(side == 1, rows, jnp.zeros_like(rows)))
        picked = jnp.concatenate(
            [jnp.concatenate(first, axis=1), jnp.concatenate(second, axis=1)], axis=0
        )
        stacked = tiles[pl.ds(s * cap, cap)].reshape(cap * tile, tile)
        return jnp.dot(picked, stacked, preferred_element_type=F32)

    index = 0
    for dist in range(half, -1, -1):
        if dist == half:
            entries = [(half, 0, [], 0), (half, 1, [], 1)]
            if half > 1:
                entries += [(half - 1, 1, [], 0), (1 - half, 0, [], 1)]
        elif dist == half - 1 and dist >= 1:
            entries = [(dist, 0, [0], 0), (-dist, 1, [1], 1)]
        elif dist >= 1:
            entries = [
                (zoff, y, [way], way) for y in range(2) for way, zoff in enumerate((dist, -dist))
            ]
        else:
            entries = [(0, 1, [0, 1] if half > 1 else [1], None)]
        if dist == min(2, half):
            entries.append((0, 0, [], None))
        units = [(index + i, zoff, yh if y else other_y) for i, (zoff, y, _, _) in enumerate(entries)]
        index += len(entries)
        for i, zoff, y in units:
            encode(sib_out.at[i], backward_unit(z_unit(zoff, y, 1 - core)))
            send(sib_out.at[i], sib_in.at[i], sib_send.at[i], sib_recv.at[i], sib, r)
        for i, zoff, y in units:
            own_sum[i] = backward_unit(z_unit(zoff, y, core))
        if dist < half - 1 and w_done[0] < 3:
            w_stage(w_done[0])
        if dist == 0:
            settle(8)
        for i, _, _ in units:
            arrived(sib_in.at[i], sib_recv.at[i])
            own_sum[i] = own_sum[i] + decode(sib_in.at[i])
        for (i, _, _), (zoff, y, ways, way) in zip(units, entries):
            value = own_sum[i]
            for w in ways:
                arrived(z_in.at[w, abs(zoff), y], z_recv.at[w, abs(zoff), y])
                value = value + decode(z_in.at[w, abs(zoff), y])
            if zoff == 0 and y == 1:
                for k in range(3):
                    arrived(y_in.at[k], y_recv.at[k])
                    value = value + decode(y_in.at[k])
                grad_out[...] = value
                continue
            out = z_out.at[i]
            encode(out, value)
            if zoff == 0:
                target, place, flag = partner, y_in.at[2], y_recv.at[2]
            elif abs(zoff) == 1 and y == 0:
                target = partner_up if way == 0 else partner_down
                place, flag = y_in.at[way], y_recv.at[way]
            else:
                target = up if way == 0 else down
                near = abs(zoff) - 1
                place, flag = z_in.at[way, near, y], z_recv.at[way, near, y]
            send(out, place, z_send.at[i], flag, target, r)
        if dist == half:
            w_stage(0)
    for stage in range(w_done[0], 4):
        w_stage(stage)

    settle()


def finish(act, grad_t, wgrad, act_out, grad_out, wgrad_out):
    act_out[...] = act[...]
    wgrad_out[...] = wgrad[...]
    feat = wgrad.shape[0]
    tile = grad_t.shape[1]
    for j in range(2):
        grad_out[j * tile:(j + 1) * tile] = grad_t[j * feat:(j + 1) * feat].T


def body(features, adj_tiles, tile_counts, dst_tile, src_tile, weight, bias_term, cotangent):
    blocks = lax.axis_size("blk")
    reps = lax.axis_size("rep")
    steps, cap, tile = adj_tiles.shape[2:5]
    rows, feat = features.shape
    node_total = rows * blocks * reps
    n_slots = steps * cap
    nz = blocks // 4
    half = nz // 2
    w_rows = feat // reps
    dst = dst_tile[0, 0].T
    src = src_tile[0, 0].T
    shapes = (
        jax.ShapeDtypeStruct((rows, feat), F32),
        jax.ShapeDtypeStruct((rows, feat), F32),
        jax.ShapeDtypeStruct((feat, feat), F32),
    )
    vmem = pl.BlockSpec(memory_space=pltpu.VMEM)
    dma = pltpu.SemaphoreType.DMA
    act, grad_t, wgrad = pl.pallas_call(
        functools.partial(kernel, blocks, reps, node_total),
        out_shape=shapes,
        in_specs=[pl.BlockSpec(memory_space=pltpu.HBM)] * 8,
        out_specs=(vmem, vmem, vmem),
        scratch_shapes=[
            pltpu.SMEM((blocks,), jnp.int32),
            pltpu.SMEM((cap, blocks), jnp.int32),
            pltpu.SMEM((cap, blocks), jnp.int32),
            pltpu.VMEM((cap, blocks), jnp.int32),
            pltpu.VMEM((feat, feat), F32),
            pltpu.VMEM((1, feat), F32),
            pltpu.VMEM((rows, feat), F32),
            pltpu.VMEM((n_slots, tile, tile), BF16),
            pltpu.VMEM((blocks, rows, feat), BF16),
            pltpu.VMEM((n_slots + 1, tile, feat), F32),
            pltpu.VMEM((16, 128), jnp.int32),
            pltpu.SMEM((16, 128), jnp.int32),
            pltpu.VMEM((reps, 2, tile + SCALE_ROWS, feat), I16),
            pltpu.VMEM((reps, 2, tile + SCALE_ROWS, feat), I16),
            pltpu.VMEM((2 * reps, feat, tile), BF16),
            pltpu.VMEM((feat, feat), F32),
            pltpu.VMEM((reps, w_rows, feat), F32),
            pltpu.VMEM((4, w_rows, feat), F32),
            pltpu.VMEM((nz, w_rows, feat), F32),
            pltpu.VMEM((reps, w_rows, feat), F32),
            pltpu.VMEM((blocks // 2, 2 * feat + SCALE_ROWS, tile), I16),
            pltpu.VMEM((blocks // 2, 2 * feat + SCALE_ROWS, tile), I16),
            pltpu.VMEM((blocks // 2, 2 * feat, tile), F32),
            pltpu.VMEM((blocks // 2, 2 * feat + SCALE_ROWS, tile), I16),
            pltpu.VMEM((2, half, 2, 2 * feat + SCALE_ROWS, tile), I16),
            pltpu.VMEM((3, 2 * feat + SCALE_ROWS, tile), I16),
            dma((8,)), dma, dma,
            dma((PIECES * 2 * blocks,)), dma((blocks, PIECES)),
            dma((reps, 2)), dma((reps, 2)),
            dma((reps, 2)), dma((reps, 2)),
            dma((2 * reps + nz + 4,)), dma((reps,)), dma((4,)), dma((nz,)), dma((reps,)),
            dma((blocks // 2,)), dma((blocks // 2,)),
            dma((blocks // 2,)), dma((2, half, 2)),
            dma((3,)),
        ],
        compiler_params=pltpu.CompilerParams(
            collective_id=0, has_side_effects=True, vmem_limit_bytes=58 * 1024 * 1024
        ),
        cost_estimate=pl.CostEstimate(
            flops=4 * n_slots * tile * tile * feat,
            bytes_accessed=n_slots * tile * tile * 2,
            transcendentals=rows * feat,
        ),
        name="graph_layer",
    )(
        features, adj_tiles.reshape(n_slots, tile, tile), tile_counts[0, 0], dst, src,
        weight, bias_term.reshape(1, feat), cotangent,
    )
    return pl.pallas_call(finish, out_shape=shapes, name="outputs")(act, grad_t, wgrad)


def solution(mesh):
    in_specs = (
        P(("blk", "rep"), None),
        P("blk", "rep", None, None, None, None),
        P("blk", "rep", None),
        P("blk", "rep", None, None),
        P("blk", "rep", None, None),
        P(),
        P(),
        P(("blk", "rep"), None),
    )
    out_specs = (P(("blk", "rep"), None), P(("blk", "rep"), None), P())
    return jax.shard_map(body, mesh=mesh, in_specs=in_specs, out_specs=out_specs, check_vma=False)
```

```python
import functools
import math

import jax
import jax.numpy as jnp
from jax import lax
from jax.experimental import pallas as pl
from jax.experimental.pallas import tpu as pltpu
from jax.sharding import PartitionSpec as P

MESH = pl.DeviceIdType.MESH
F32 = jnp.float32
BF16 = jnp.bfloat16
HIGHEST = lax.Precision.HIGHEST
I16 = jnp.int16
SCALE_ROWS = 16
PIECES = 1


def encode(ref, value):
    rows = value.shape[0]
    largest = jnp.max(jnp.abs(value), axis=0, keepdims=True)
    power = jnp.clip(jnp.floor(14.9 - jnp.log2(largest)), -120.0, 120.0)
    ref[0:rows] = jnp.round(value * jnp.exp2(power)).astype(jnp.int32).astype(I16)
    ref[rows:rows + SCALE_ROWS] = jnp.broadcast_to(
        power.astype(jnp.int32), (SCALE_ROWS, value.shape[1])
    ).astype(I16)


def decode(ref):
    rows = ref.shape[0] - SCALE_ROWS
    scale = jnp.exp2(-ref[rows:rows + SCALE_ROWS].astype(jnp.int32).astype(F32))
    value = ref[0:rows].astype(jnp.int32).astype(F32)
    grouped = value.reshape(rows // SCALE_ROWS, SCALE_ROWS, value.shape[1]) * scale[None]
    return grouped.reshape(value.shape)


def kernel(
    blocks, reps, node_total,
    features, tiles_hbm, counts_hbm, dst_hbm, src_hbm, weight_hbm, bias_hbm, cotangent_hbm,
    act_out, grad_out, wgrad_out,
    counts, dst, src, dst_vec, weight, bias, cotangent, tiles, feats, chain, links_vec, links,
    part, part_in, grads_t, wterm, wrep, wquad, wz, wall,
    sib_out, sib_in, own_sum, z_out, z_in, y_in,
    in_sems, tile_sem, link_sem, ag_send, ag_recv, rs_send, rs_recv, g_send, g_recv,
    w_send, w1_recv, w2_recv, w3_recv, w4_recv,
    sib_send, sib_recv, z_send, z_recv, y_recv,
):
    nz = blocks // 4
    half = nz // 2
    cap = dst.shape[0]
    tile = tiles.shape[1]
    feat = features.shape[1]
    n_slots = blocks * cap
    b = lax.axis_index("blk")
    r = lax.axis_index("rep")
    core = lax.rem(b, 2)
    yh = lax.rem(b // 2, 2)
    z = b // 4
    sib = b + 1 - 2 * core
    partner = b + 2 - 4 * yh
    diag = sib + 2 - 4 * yh
    up = lax.rem(b + 4, blocks)
    down = lax.rem(b + blocks - 4, blocks)

    sent = []

    def send(src_ref, dst_ref, send_sem, recv_sem, blk, rep):
        copy = pltpu.make_async_remote_copy(
            src_ref=src_ref, dst_ref=dst_ref, send_sem=send_sem, recv_sem=recv_sem,
            device_id=(blk, rep), device_id_type=MESH,
        )
        copy.start()
        sent.append(copy)

    def settle(keep=0):
        while len(sent) > keep:
            sent.pop(0).wait_send()

    def arrived(dst_ref, recv_sem):
        pltpu.make_async_remote_copy(
            src_ref=dst_ref, dst_ref=dst_ref, send_sem=w_send.at[0], recv_sem=recv_sem,
            device_id=(sib, r), device_id_type=MESH,
        ).wait_recv()

    z_peers = [lax.rem(b + 4 * i, blocks) for i in range(1, nz)]
    n_x = reps // 2
    steps_away = sorted(
        ((dx, dy) for dx in range(n_x) for dy in range(2) if dx + dy),
        key=lambda step: (-min(step[0], n_x - step[0]) - step[1], -step[1], step[0]),
    )
    rep_peers = [
        lax.rem(r // n_x + dy, 2) * n_x + lax.rem(lax.rem(r, n_x) + dx, n_x) for dx, dy in steps_away
    ]
    partner_up = lax.rem(partner + 4, blocks)
    partner_down = lax.rem(partner + blocks - 4, blocks)
    blk_peers = [sib, partner, diag, partner_up, partner_down] + z_peers
    barrier = pltpu.get_barrier_semaphore()
    for blk in blk_peers:
        pl.semaphore_signal(barrier, inc=1, device_id=(blk, r), device_id_type=MESH)
    for rep in rep_peers:
        pl.semaphore_signal(barrier, inc=1, device_id=(b, rep), device_id_type=MESH)
    copies = [
        pltpu.make_async_copy(from_ref, to_ref, in_sems.at[i])
        for i, (from_ref, to_ref) in enumerate([
            (features, feats.at[b]), (dst_hbm, dst_vec), (dst_hbm, dst), (counts_hbm, counts),
            (src_hbm, src), (weight_hbm, weight), (bias_hbm, bias), (cotangent_hbm, cotangent),
        ])
    ]
    own_copy, index_copies, dense_copies = copies[0], copies[1:5], copies[5:]
    own_copy.start()
    for copy in index_copies:
        copy.start()
    tile_copy = pltpu.make_async_copy(tiles_hbm, tiles, tile_sem)
    tile_copy.start()
    for copy in dense_copies:
        copy.start()
    pl.semaphore_wait(barrier, len(blk_peers) + len(rep_peers))

    ag_count = [0]
    piece = features.shape[0] // PIECES

    def pass_on(u, target, first, n_rows, flag):
        rows = feats.at[u, pl.ds(first, n_rows)]
        send(rows, rows, ag_send.at[ag_count[0]], ag_recv.at[u, flag], target, r)
        ag_count[0] += 1

    def to_sibling(u):
        pass_on(u, sib, 0, PIECES * piece, 0)

    def unit_arrived(u):
        arrived(feats.at[u], ag_recv.at[u, 0])

    own_copy.wait()
    for targets in ((up, down), (partner_up, partner_down, partner)):
        for h in range(PIECES):
            for target in targets:
                pass_on(b, target, h * piece, piece, h)
    to_sibling(b)
    for copy in index_copies:
        copy.wait()

    groups = [("own", 0)]
    for d in range(1, half + 1):
        groups += [("own", d), ("other", d)]
        if d == 1:
            groups.append(("other", 0))

    def group_size(group):
        return 2 if group[1] in (0, half) else 4

    starts = {}
    total_steps = 0
    for group in groups:
        starts[group] = total_steps
        total_steps += group_size(group)

    def unit_in(group, j):
        which, d = group
        y = yh if which == "own" else 1 - yh
        if group_size(group) == 2:
            zoff, c = d, j
        else:
            zoff, c = nz + d * (2 * lax.rem(j, 2) - 1), j // 2
        return lax.rem(z + zoff, nz) * 4 + 2 * y + lax.rem(core + c, 2)

    dst_tab = dst_vec[...]
    slot_iota = lax.broadcasted_iota(jnp.int32, dst_tab.shape, 1) * cap + lax.broadcasted_iota(
        jnp.int32, dst_tab.shape, 0
    )
    tile_iota = lax.broadcasted_iota(jnp.int32, (8, 128), 1)

    def link_step(group, j, carry):
        current, before, last = carry
        n = starts[group] + j
        s = lax.rem(b - unit_in(group, j) + blocks, blocks)
        for k in range(cap):
            to = jnp.where(k < counts[s], dst[k, s], -1)
            before = jnp.where(slot_iota == s * cap + k, current, before)
            current = jnp.where(dst_tab == to, n * cap + k, current)
            last = jnp.where(tile_iota == to, n * cap + k, last)
        return current, before, last

    nothing = jnp.full(dst_tab.shape, n_slots, jnp.int32)
    carry = (nothing, nothing, jnp.full((8, 128), n_slots, jnp.int32))
    for group in groups:
        carry = lax.fori_loop(0, group_size(group), functools.partial(link_step, group), carry)
    _, before, last = carry
    links_vec[...] = jnp.zeros(links_vec.shape, jnp.int32)
    links_vec[0:cap, 0:blocks] = before
    links_vec[8:16, :] = last
    link_copy = pltpu.make_async_copy(links_vec, links, link_sem)
    link_copy.start()
    chain[n_slots] = jnp.zeros((tile, feat), F32)

    other_y = 1 - yh
    z_base = {zoff: lax.rem(z + zoff + nz, nz) * 4 for zoff in range(1 - half, half + 1)}

    def z_unit(zoff, y, c):
        return z_base[zoff] + 2 * y + c

    def take_in(group):
        which, d = group
        y = yh if which == "own" else other_y
        if d in (0, half):
            moves = [(d, None)]
        else:
            moves = [
                (zoff, target if d + 1 < half or which == last_y else None)
                for zoff, target, last_y in ((-d, up, "own"), (d, down, "other"))
            ]
        for h in range(PIECES):
            for zoff, target in moves:
                u = z_unit(zoff, y, core)
                arrived(feats.at[u, pl.ds(h * piece, piece)], ag_recv.at[u, h])
                if target is not None:
                    pass_on(u, target, h * piece, piece, h)
        for zoff, _ in moves:
            to_sibling(z_unit(zoff, y, core))

    def work_on(group):
        which, d = group
        y = yh if which == "own" else other_y
        for zoff in (d,) if d in (0, half) else (-d, d):
            unit_arrived(z_unit(zoff, y, 1 - core))

        def one(j, carry):
            u = unit_in(group, j)
            n = starts[group] + j
            s = lax.rem(b - u + blocks, blocks)
            seen = feats[u]
            both = jnp.concatenate([seen[:tile], seen[tile:]], axis=1)
            for k in range(cap):
                product = jnp.dot(tiles[s * cap + k], both, preferred_element_type=F32)
                use_second = jnp.full((tile, feat), src[k, s], jnp.int32) == 1
                term = jnp.where(use_second, product[:, feat:], product[:, :feat])
                chain[n * cap + k] = term + chain[links[k, s]]
            return carry

        lax.fori_loop(0, group_size(group), one, 0)

    for i, group in enumerate(groups):
        if i == len(groups) - 1:
            work_on(groups[i - 2])
        if i >= 1:
            take_in(group)
        if i == 1:
            link_copy.wait()
            tile_copy.wait()
        if 2 <= i < len(groups) - 1:
            work_on(groups[i - 2])
    work_on(groups[-2])
    work_on(groups[-1])

    def partial_of(t):
        return chain[links[8, t]]

    for j in range(2):
        for i, rep in enumerate(rep_peers):
            encode(part.at[rep, j], partial_of(rep * 2 + j))
            send(part.at[rep, j], part_in.at[r, j], rs_send.at[i, j], rs_recv.at[r, j], b, rep)
    settle(2 * len(rep_peers))
    for copy in dense_copies:
        copy.wait()
    terms = []
    for j in range(2):
        aggregate = partial_of(r * 2 + j)
        for rep in rep_peers:
            arrived(part_in.at[rep, j], rs_recv.at[rep, j])
            aggregate = aggregate + decode(part_in.at[rep, j])
        rows = slice(j * tile, (j + 1) * tile)
        pre_act = jnp.dot(
            aggregate, weight[...], precision=HIGHEST, preferred_element_type=F32
        ) + bias[...]
        sigma = jax.nn.sigmoid(pre_act)
        pre_grad = cotangent[rows] * sigma * (1.0 + pre_act * (1.0 - sigma))
        grads_t[2 * r + j] = lax.dot_general(
            weight[...], pre_grad, (((1,), (1,)), ((), ())),
            precision=HIGHEST, preferred_element_type=F32,
        ).astype(BF16)
        mine = grads_t.at[2 * r + j]
        for i, rep in enumerate(rep_peers):
            send(mine, mine, g_send.at[i, j], g_recv.at[r, j], b, rep)
        act_out[rows] = pre_act * sigma
        terms.append((aggregate, pre_grad))

    wterm[...] = sum(
        lax.dot_general(
            aggregate, pre_grad, (((0,), (0,)), ((), ())), precision=HIGHEST, preferred_element_type=F32
        )
        for aggregate, pre_grad in terms
    ) * (1.0 / math.sqrt(node_total))
    w_rows = feat // reps
    w_count = [0]

    def w_send_to(src_ref, dst_ref, recv_sem, blk, rep):
        send(src_ref, dst_ref, w_send.at[w_count[0]], recv_sem, blk, rep)
        w_count[0] += 1

    for rep in rep_peers:
        w_send_to(wterm.at[pl.ds(rep * w_rows, w_rows)], wrep.at[r], w1_recv.at[r], b, rep)
    settle(3 * len(rep_peers))
    for rep in rep_peers:
        for j in range(2):
            arrived(grads_t.at[2 * rep + j], g_recv.at[rep, j])

    w_done = [0]

    def w_stage(stage):
        w_done[0] += 1
        if stage == 0:
            total = wterm[pl.ds(r * w_rows, w_rows)]
            for rep in rep_peers:
                arrived(wrep.at[rep], w1_recv.at[rep])
                total = total + wrep[rep]
            place = lax.rem(b, 4)
            wquad[place] = total
            for blk in [sib, partner, diag]:
                w_send_to(wquad.at[place], wquad.at[place], w2_recv.at[place], blk, r)
        elif stage == 1:
            for blk in [sib, partner, diag]:
                place = lax.rem(blk, 4)
                arrived(wquad.at[place], w2_recv.at[place])
            total = wquad[0]
            for i in range(1, 4):
                total = total + wquad[i]
            wz[z] = total
            for blk in z_peers:
                w_send_to(wz.at[z], wz.at[z], w3_recv.at[z], blk, r)
        elif stage == 2:
            for blk in z_peers:
                arrived(wz.at[blk // 4], w3_recv.at[blk // 4])
            total = wz[0]
            for i in range(1, nz):
                total = total + wz[i]
            wall[r] = total
            for rep in rep_peers:
                w_send_to(wall.at[r], wall.at[r], w4_recv.at[r], b, rep)
        else:
            for rep in rep_peers:
                arrived(wall.at[rep], w4_recv.at[rep])
            wgrad_out[...] = wall[...].reshape(feat, feat)

    def backward_unit(u):
        s = lax.rem(b - u + blocks, blocks)
        first, second = [], []
        for k in range(cap):
            rows = grads_t[dst[k, s]]
            side = jnp.full(rows.shape, jnp.where(k < counts[s], src[k, s], 2), jnp.int32)
            first.append(jnp.where(side == 0, rows, jnp.zeros_like(rows)))
            second.append(jnp.where(side == 1, rows, jnp.zeros_like(rows)))
        picked = jnp.concatenate(
            [jnp.concatenate(first, axis=1), jnp.concatenate(second, axis=1)], axis=0
        )
        stacked = tiles[pl.ds(s * cap, cap)].reshape(cap * tile, tile)
        return jnp.dot(picked, stacked, preferred_element_type=F32)

    index = 0
    for dist in range(half, -1, -1):
        if dist == half:
            entries = [(half, 0, [], 0), (half, 1, [], 1)]
            if half > 1:
                entries += [(half - 1, 1, [], 0), (1 - half, 0, [], 1)]
        elif dist == half - 1 and dist >= 1:
            entries = [(dist, 0, [0], 0), (-dist, 1, [1], 1)]
        elif dist >= 1:
            entries = [
                (zoff, y, [way], way) for y in range(2) for way, zoff in enumerate((dist, -dist))
            ]
        else:
            entries = [(0, 1, [0, 1] if half > 1 else [1], None)]
        if dist == min(2, half):
            entries.append((0, 0, [], None))
        units = [(index + i, zoff, yh if y else other_y) for i, (zoff, y, _, _) in enumerate(entries)]
        index += len(entries)
        for i, zoff, y in units:
            encode(sib_out.at[i], backward_unit(z_unit(zoff, y, 1 - core)))
            send(sib_out.at[i], sib_in.at[i], sib_send.at[i], sib_recv.at[i], sib, r)
        if dist < half - 1 and w_done[0] < 3:
            w_stage(w_done[0])
        if dist == 0:
            settle(8)
        batch = 2 if dist == half else len(units)
        ready = 0
        for (i, _, _), (zoff, y, ways, way) in zip(units, entries):
            if ready == 0:
                ready = batch
                coming = units[i - units[0][0]:][:batch]
                for m, m_zoff, m_y in coming:
                    own_sum[m] = backward_unit(z_unit(m_zoff, m_y, core))
                for m, _, _ in coming:
                    arrived(sib_in.at[m], sib_recv.at[m])
                    own_sum[m] = own_sum[m] + decode(sib_in.at[m])
            ready -= 1
            value = own_sum[i]
            for w in ways:
                arrived(z_in.at[w, abs(zoff), y], z_recv.at[w, abs(zoff), y])
                value = value + decode(z_in.at[w, abs(zoff), y])
            if zoff == 0 and y == 1:
                for k in range(3):
                    arrived(y_in.at[k], y_recv.at[k])
                    value = value + decode(y_in.at[k])
                grad_out[...] = value
                continue
            out = z_out.at[i]
            encode(out, value)
            if zoff == 0:
                target, place, flag = partner, y_in.at[2], y_recv.at[2]
            elif abs(zoff) == 1 and y == 0:
                target = partner_up if way == 0 else partner_down
                place, flag = y_in.at[way], y_recv.at[way]
            else:
                target = up if way == 0 else down
                near = abs(zoff) - 1
                place, flag = z_in.at[way, near, y], z_recv.at[way, near, y]
            send(out, place, z_send.at[i], flag, target, r)
        if dist == half:
            w_stage(0)
    for stage in range(w_done[0], 4):
        w_stage(stage)

    settle()


def finish(act, grad_t, wgrad, act_out, grad_out, wgrad_out):
    act_out[...] = act[...]
    wgrad_out[...] = wgrad[...]
    feat = wgrad.shape[0]
    tile = grad_t.shape[1]
    for j in range(2):
        grad_out[j * tile:(j + 1) * tile] = grad_t[j * feat:(j + 1) * feat].T


def body(features, adj_tiles, tile_counts, dst_tile, src_tile, weight, bias_term, cotangent):
    blocks = lax.axis_size("blk")
    reps = lax.axis_size("rep")
    steps, cap, tile = adj_tiles.shape[2:5]
    rows, feat = features.shape
    node_total = rows * blocks * reps
    n_slots = steps * cap
    nz = blocks // 4
    half = nz // 2
    w_rows = feat // reps
    dst = dst_tile[0, 0].T
    src = src_tile[0, 0].T
    shapes = (
        jax.ShapeDtypeStruct((rows, feat), F32),
        jax.ShapeDtypeStruct((rows, feat), F32),
        jax.ShapeDtypeStruct((feat, feat), F32),
    )
    vmem = pl.BlockSpec(memory_space=pltpu.VMEM)
    dma = pltpu.SemaphoreType.DMA
    act, grad_t, wgrad = pl.pallas_call(
        functools.partial(kernel, blocks, reps, node_total),
        out_shape=shapes,
        in_specs=[pl.BlockSpec(memory_space=pltpu.HBM)] * 8,
        out_specs=(vmem, vmem, vmem),
        scratch_shapes=[
            pltpu.SMEM((blocks,), jnp.int32),
            pltpu.SMEM((cap, blocks), jnp.int32),
            pltpu.SMEM((cap, blocks), jnp.int32),
            pltpu.VMEM((cap, blocks), jnp.int32),
            pltpu.VMEM((feat, feat), F32),
            pltpu.VMEM((1, feat), F32),
            pltpu.VMEM((rows, feat), F32),
            pltpu.VMEM((n_slots, tile, tile), BF16),
            pltpu.VMEM((blocks, rows, feat), BF16),
            pltpu.VMEM((n_slots + 1, tile, feat), F32),
            pltpu.VMEM((16, 128), jnp.int32),
            pltpu.SMEM((16, 128), jnp.int32),
            pltpu.VMEM((reps, 2, tile + SCALE_ROWS, feat), I16),
            pltpu.VMEM((reps, 2, tile + SCALE_ROWS, feat), I16),
            pltpu.VMEM((2 * reps, feat, tile), BF16),
            pltpu.VMEM((feat, feat), F32),
            pltpu.VMEM((reps, w_rows, feat), F32),
            pltpu.VMEM((4, w_rows, feat), F32),
            pltpu.VMEM((nz, w_rows, feat), F32),
            pltpu.VMEM((reps, w_rows, feat), F32),
            pltpu.VMEM((blocks // 2, 2 * feat + SCALE_ROWS, tile), I16),
            pltpu.VMEM((blocks // 2, 2 * feat + SCALE_ROWS, tile), I16),
            pltpu.VMEM((blocks // 2, 2 * feat, tile), F32),
            pltpu.VMEM((blocks // 2, 2 * feat + SCALE_ROWS, tile), I16),
            pltpu.VMEM((2, half, 2, 2 * feat + SCALE_ROWS, tile), I16),
            pltpu.VMEM((3, 2 * feat + SCALE_ROWS, tile), I16),
            dma((8,)), dma, dma,
            dma((PIECES * 2 * blocks,)), dma((blocks, PIECES)),
            dma((reps, 2)), dma((reps, 2)),
            dma((reps, 2)), dma((reps, 2)),
            dma((2 * reps + nz + 4,)), dma((reps,)), dma((4,)), dma((nz,)), dma((reps,)),
            dma((blocks // 2,)), dma((blocks // 2,)),
            dma((blocks // 2,)), dma((2, half, 2)),
            dma((3,)),
        ],
        compiler_params=pltpu.CompilerParams(
            collective_id=0, has_side_effects=True, vmem_limit_bytes=58 * 1024 * 1024
        ),
        cost_estimate=pl.CostEstimate(
            flops=4 * n_slots * tile * tile * feat,
            bytes_accessed=n_slots * tile * tile * 2,
            transcendentals=rows * feat,
        ),
        name="graph_layer",
    )(
        features, adj_tiles.reshape(n_slots, tile, tile), tile_counts[0, 0], dst, src,
        weight, bias_term.reshape(1, feat), cotangent,
    )
    return pl.pallas_call(finish, out_shape=shapes, name="outputs")(act, grad_t, wgrad)


def solution(mesh):
    in_specs = (
        P(("blk", "rep"), None),
        P("blk", "rep", None, None, None, None),
        P("blk", "rep", None),
        P("blk", "rep", None, None),
        P("blk", "rep", None, None),
        P(),
        P(),
        P(("blk", "rep"), None),
    )
    out_specs = (P(("blk", "rep"), None), P(("blk", "rep"), None), P())
    return jax.shard_map(body, mesh=mesh, in_specs=in_specs, out_specs=out_specs, check_vma=False)
```

```python
import functools
import math

import jax
import jax.numpy as jnp
from jax import lax
from jax.experimental import pallas as pl
from jax.experimental.pallas import tpu as pltpu
from jax.sharding import PartitionSpec as P

MESH = pl.DeviceIdType.MESH
F32 = jnp.float32
BF16 = jnp.bfloat16
HIGHEST = lax.Precision.HIGHEST
I16 = jnp.int16
SCALE_ROWS = 16
PIECES = 1


def encode(ref, value):
    rows = value.shape[0]
    largest = jnp.max(jnp.abs(value), axis=0, keepdims=True)
    power = jnp.clip(jnp.floor(14.9 - jnp.log2(largest)), -120.0, 120.0)
    ref[0:rows] = jnp.round(value * jnp.exp2(power)).astype(jnp.int32).astype(I16)
    ref[rows:rows + SCALE_ROWS] = jnp.broadcast_to(
        power.astype(jnp.int32), (SCALE_ROWS, value.shape[1])
    ).astype(I16)


def decode(ref):
    rows = ref.shape[0] - SCALE_ROWS
    scale = jnp.exp2(-ref[rows:rows + SCALE_ROWS].astype(jnp.int32).astype(F32))
    value = ref[0:rows].astype(jnp.int32).astype(F32)
    grouped = value.reshape(rows // SCALE_ROWS, SCALE_ROWS, value.shape[1]) * scale[None]
    return grouped.reshape(value.shape)


def kernel(
    blocks, reps, node_total,
    features, tiles_hbm, counts_hbm, dst_hbm, src_hbm, weight_hbm, bias_hbm, cotangent_hbm,
    act_out, grad_out, wgrad_out,
    counts, dst, src, dst_vec, weight, bias, cotangent, tiles, feats, chain, links_vec, links,
    part, part_in, grads_t, wterm, wrep, wquad, wz, wall,
    sib_out, sib_in, own_sum, z_out, z_in, y_in,
    in_sems, tile_sem, link_sem, ag_send, ag_recv, rs_send, rs_recv, g_send, g_recv,
    w_send, w1_recv, w2_recv, w3_recv, w4_recv,
    sib_send, sib_recv, z_send, z_recv, y_recv,
):
    nz = blocks // 4
    half = nz // 2
    cap = dst.shape[0]
    tile = tiles.shape[1]
    feat = features.shape[1]
    n_slots = blocks * cap
    b = lax.axis_index("blk")
    r = lax.axis_index("rep")
    core = lax.rem(b, 2)
    yh = lax.rem(b // 2, 2)
    z = b // 4
    sib = b + 1 - 2 * core
    partner = b + 2 - 4 * yh
    diag = sib + 2 - 4 * yh
    up = lax.rem(b + 4, blocks)
    down = lax.rem(b + blocks - 4, blocks)

    sent = []

    def send(src_ref, dst_ref, send_sem, recv_sem, blk, rep):
        copy = pltpu.make_async_remote_copy(
            src_ref=src_ref, dst_ref=dst_ref, send_sem=send_sem, recv_sem=recv_sem,
            device_id=(blk, rep), device_id_type=MESH,
        )
        copy.start()
        sent.append(copy)

    def settle(keep=0):
        while len(sent) > keep:
            sent.pop(0).wait_send()

    def arrived(dst_ref, recv_sem):
        pltpu.make_async_remote_copy(
            src_ref=dst_ref, dst_ref=dst_ref, send_sem=w_send.at[0], recv_sem=recv_sem,
            device_id=(sib, r), device_id_type=MESH,
        ).wait_recv()

    z_peers = [lax.rem(b + 4 * i, blocks) for i in range(1, nz)]
    n_x = reps // 2
    steps_away = sorted(
        ((dx, dy) for dx in range(n_x) for dy in range(2) if dx + dy),
        key=lambda step: (-min(step[0], n_x - step[0]) - step[1], -step[1], step[0]),
    )
    rep_peers = [
        lax.rem(r // n_x + dy, 2) * n_x + lax.rem(lax.rem(r, n_x) + dx, n_x) for dx, dy in steps_away
    ]
    partner_up = lax.rem(partner + 4, blocks)
    partner_down = lax.rem(partner + blocks - 4, blocks)
    blk_peers = [sib, partner, diag, partner_up, partner_down] + z_peers
    barrier = pltpu.get_barrier_semaphore()
    for blk in blk_peers:
        pl.semaphore_signal(barrier, inc=1, device_id=(blk, r), device_id_type=MESH)
    for rep in rep_peers:
        pl.semaphore_signal(barrier, inc=1, device_id=(b, rep), device_id_type=MESH)
    copies = [
        pltpu.make_async_copy(from_ref, to_ref, in_sems.at[i])
        for i, (from_ref, to_ref) in enumerate([
            (features, feats.at[b]), (dst_hbm, dst_vec), (dst_hbm, dst), (counts_hbm, counts),
            (src_hbm, src), (weight_hbm, weight), (bias_hbm, bias), (cotangent_hbm, cotangent),
        ])
    ]
    own_copy, index_copies, dense_copies = copies[0], copies[1:5], copies[5:]
    own_copy.start()
    for copy in index_copies:
        copy.start()
    tile_copy = pltpu.make_async_copy(tiles_hbm, tiles, tile_sem)
    tile_copy.start()
    for copy in dense_copies:
        copy.start()
    pl.semaphore_wait(barrier, len(blk_peers) + len(rep_peers))

    ag_count = [0]
    piece = features.shape[0] // PIECES

    def pass_on(u, target, first, n_rows, flag):
        rows = feats.at[u, pl.ds(first, n_rows)]
        send(rows, rows, ag_send.at[ag_count[0]], ag_recv.at[u, flag], target, r)
        ag_count[0] += 1

    def to_sibling(u):
        pass_on(u, sib, 0, PIECES * piece, 0)

    def unit_arrived(u):
        arrived(feats.at[u], ag_recv.at[u, 0])

    own_copy.wait()
    for targets in ((up, down), (partner_up, partner_down, partner)):
        for h in range(PIECES):
            for target in targets:
                pass_on(b, target, h * piece, piece, h)
    to_sibling(b)
    for copy in index_copies:
        copy.wait()

    groups = [("own", 0)]
    for d in range(1, half + 1):
        groups += [("own", d), ("other", d)]
        if d == 1:
            groups.append(("other", 0))

    def group_size(group):
        return 2 if group[1] in (0, half) else 4

    starts = {}
    total_steps = 0
    for group in groups:
        starts[group] = total_steps
        total_steps += group_size(group)

    def unit_in(group, j):
        which, d = group
        y = yh if which == "own" else 1 - yh
        if group_size(group) == 2:
            zoff, c = d, j
        else:
            zoff, c = nz + d * (2 * lax.rem(j, 2) - 1), j // 2
        return lax.rem(z + zoff, nz) * 4 + 2 * y + lax.rem(core + c, 2)

    dst_tab = dst_vec[...]
    slot_iota = lax.broadcasted_iota(jnp.int32, dst_tab.shape, 1) * cap + lax.broadcasted_iota(
        jnp.int32, dst_tab.shape, 0
    )
    tile_iota = lax.broadcasted_iota(jnp.int32, (8, 128), 1)

    def link_step(group, j, carry):
        current, before, last = carry
        n = starts[group] + j
        s = lax.rem(b - unit_in(group, j) + blocks, blocks)
        for k in range(cap):
            to = jnp.where(k < counts[s], dst[k, s], -1)
            before = jnp.where(slot_iota == s * cap + k, current, before)
            current = jnp.where(dst_tab == to, n * cap + k, current)
            last = jnp.where(tile_iota == to, n * cap + k, last)
        return current, before, last

    nothing = jnp.full(dst_tab.shape, n_slots, jnp.int32)
    carry = (nothing, nothing, jnp.full((8, 128), n_slots, jnp.int32))
    for group in groups:
        carry = lax.fori_loop(0, group_size(group), functools.partial(link_step, group), carry)
    _, before, last = carry
    links_vec[...] = jnp.zeros(links_vec.shape, jnp.int32)
    links_vec[0:cap, 0:blocks] = before
    links_vec[8:16, :] = last
    link_copy = pltpu.make_async_copy(links_vec, links, link_sem)
    link_copy.start()
    chain[n_slots] = jnp.zeros((tile, feat), F32)

    other_y = 1 - yh
    z_base = {zoff: lax.rem(z + zoff + nz, nz) * 4 for zoff in range(1 - half, half + 1)}

    def z_unit(zoff, y, c):
        return z_base[zoff] + 2 * y + c

    def take_in(group):
        which, d = group
        y = yh if which == "own" else other_y
        if d in (0, half):
            moves = [(d, None)]
        else:
            moves = [
                (zoff, target if d + 1 < half or which == last_y else None)
                for zoff, target, last_y in ((-d, up, "own"), (d, down, "other"))
            ]
        for h in range(PIECES):
            for zoff, target in moves:
                u = z_unit(zoff, y, core)
                arrived(feats.at[u, pl.ds(h * piece, piece)], ag_recv.at[u, h])
                if target is not None:
                    pass_on(u, target, h * piece, piece, h)
        for zoff, _ in moves:
            to_sibling(z_unit(zoff, y, core))

    def work_on(group):
        which, d = group
        y = yh if which == "own" else other_y
        for zoff in (d,) if d in (0, half) else (-d, d):
            unit_arrived(z_unit(zoff, y, 1 - core))

        def one(j, carry):
            u = unit_in(group, j)
            n = starts[group] + j
            s = lax.rem(b - u + blocks, blocks)
            seen = feats[u]
            both = jnp.concatenate([seen[:tile], seen[tile:]], axis=1)
            for k in range(cap):
                product = jnp.dot(tiles[s * cap + k], both, preferred_element_type=F32)
                use_second = jnp.full((tile, feat), src[k, s], jnp.int32) == 1
                term = jnp.where(use_second, product[:, feat:], product[:, :feat])
                chain[n * cap + k] = term + chain[links[k, s]]
            return carry

        lax.fori_loop(0, group_size(group), one, 0)

    for i, group in enumerate(groups):
        if i == len(groups) - 1:
            work_on(groups[i - 2])
        if i >= 1:
            take_in(group)
        if i == 1:
            link_copy.wait()
            tile_copy.wait()
        if 2 <= i < len(groups) - 1:
            work_on(groups[i - 2])
    work_on(groups[-2])
    work_on(groups[-1])

    def partial_of(t):
        return chain[links[8, t]]

    for j in range(2):
        for i, rep in enumerate(rep_peers):
            encode(part.at[rep, j], partial_of(rep * 2 + j))
            send(part.at[rep, j], part_in.at[r, j], rs_send.at[i, j], rs_recv.at[r, j], b, rep)
    settle(2 * len(rep_peers))
    for copy in dense_copies:
        copy.wait()
    terms = []
    for j in range(2):
        aggregate = partial_of(r * 2 + j)
        for rep in rep_peers:
            arrived(part_in.at[rep, j], rs_recv.at[rep, j])
            aggregate = aggregate + decode(part_in.at[rep, j])
        rows = slice(j * tile, (j + 1) * tile)
        pre_act = jnp.dot(
            aggregate, weight[...], precision=HIGHEST, preferred_element_type=F32
        ) + bias[...]
        sigma = jax.nn.sigmoid(pre_act)
        pre_grad = cotangent[rows] * sigma * (1.0 + pre_act * (1.0 - sigma))
        grads_t[2 * r + j] = lax.dot_general(
            weight[...], pre_grad, (((1,), (1,)), ((), ())),
            precision=HIGHEST, preferred_element_type=F32,
        ).astype(BF16)
        mine = grads_t.at[2 * r + j]
        for i, rep in enumerate(rep_peers):
            send(mine, mine, g_send.at[i, j], g_recv.at[r, j], b, rep)
        act_out[rows] = pre_act * sigma
        terms.append((aggregate, pre_grad))

    wterm[...] = sum(
        lax.dot_general(
            aggregate, pre_grad, (((0,), (0,)), ((), ())), precision=HIGHEST, preferred_element_type=F32
        )
        for aggregate, pre_grad in terms
    ) * (1.0 / math.sqrt(node_total))
    w_rows = feat // reps
    w_count = [0]

    def w_send_to(src_ref, dst_ref, recv_sem, blk, rep):
        send(src_ref, dst_ref, w_send.at[w_count[0]], recv_sem, blk, rep)
        w_count[0] += 1

    for rep in rep_peers:
        w_send_to(wterm.at[pl.ds(rep * w_rows, w_rows)], wrep.at[r], w1_recv.at[r], b, rep)
    settle(3 * len(rep_peers))
    for rep in rep_peers:
        for j in range(2):
            arrived(grads_t.at[2 * rep + j], g_recv.at[rep, j])

    w_done = [0]

    def w_stage(stage):
        w_done[0] += 1
        if stage == 0:
            total = wterm[pl.ds(r * w_rows, w_rows)]
            for rep in rep_peers:
                arrived(wrep.at[rep], w1_recv.at[rep])
                total = total + wrep[rep]
            place = lax.rem(b, 4)
            wquad[place] = total
            for blk in [sib, partner, diag]:
                w_send_to(wquad.at[place], wquad.at[place], w2_recv.at[place], blk, r)
        elif stage == 1:
            for blk in [sib, partner, diag]:
                place = lax.rem(blk, 4)
                arrived(wquad.at[place], w2_recv.at[place])
            total = wquad[0]
            for i in range(1, 4):
                total = total + wquad[i]
            wz[z] = total
            for blk in z_peers:
                w_send_to(wz.at[z], wz.at[z], w3_recv.at[z], blk, r)
        elif stage == 2:
            for blk in z_peers:
                arrived(wz.at[blk // 4], w3_recv.at[blk // 4])
            total = wz[0]
            for i in range(1, nz):
                total = total + wz[i]
            wall[r] = total
            for rep in rep_peers:
                w_send_to(wall.at[r], wall.at[r], w4_recv.at[r], b, rep)
        else:
            for rep in rep_peers:
                arrived(wall.at[rep], w4_recv.at[rep])
            wgrad_out[...] = wall[...].reshape(feat, feat)

    def backward_unit(u):
        s = lax.rem(b - u + blocks, blocks)
        first, second = [], []
        for k in range(cap):
            rows = grads_t[dst[k, s]]
            side = jnp.full(rows.shape, jnp.where(k < counts[s], src[k, s], 2), jnp.int32)
            first.append(jnp.where(side == 0, rows, jnp.zeros_like(rows)))
            second.append(jnp.where(side == 1, rows, jnp.zeros_like(rows)))
        picked = jnp.concatenate(
            [jnp.concatenate(first, axis=1), jnp.concatenate(second, axis=1)], axis=0
        )
        stacked = tiles[pl.ds(s * cap, cap)].reshape(cap * tile, tile)
        return jnp.dot(picked, stacked, preferred_element_type=F32)

    index = 0
    for dist in range(half, -1, -1):
        if dist == half:
            entries = [(half, 0, [], 0), (half, 1, [], 1)]
            if half > 1:
                entries += [(half - 1, 1, [], 0), (1 - half, 0, [], 1)]
        elif dist == half - 1 and dist >= 1:
            entries = [(dist, 0, [0], 0), (-dist, 1, [1], 1)]
        elif dist >= 1:
            entries = [
                (zoff, y, [way], way) for y in range(2) for way, zoff in enumerate((dist, -dist))
            ]
        else:
            entries = [(0, 1, [0, 1] if half > 1 else [1], None)]
        if dist == min(2, half):
            entries.append((0, 0, [], None))
        units = [(index + i, zoff, yh if y else other_y) for i, (zoff, y, _, _) in enumerate(entries)]
        index += len(entries)
        for i, zoff, y in units:
            encode(sib_out.at[i], backward_unit(z_unit(zoff, y, 1 - core)))
            send(sib_out.at[i], sib_in.at[i], sib_send.at[i], sib_recv.at[i], sib, r)
        if dist < half - 1 and w_done[0] < 3:
            w_stage(w_done[0])
        if dist == 0:
            settle(8)
        batch = 2
        ready = 0
        for (i, _, _), (zoff, y, ways, way) in zip(units, entries):
            if ready == 0:
                ready = batch
                coming = units[i - units[0][0]:][:batch]
                for m, m_zoff, m_y in coming:
                    own_sum[m] = backward_unit(z_unit(m_zoff, m_y, core))
                for m, _, _ in coming:
                    arrived(sib_in.at[m], sib_recv.at[m])
                    own_sum[m] = own_sum[m] + decode(sib_in.at[m])
            ready -= 1
            value = own_sum[i]
            if zoff == 0 and y == 1:
                for k in (2, 0, 1):
                    arrived(y_in.at[k], y_recv.at[k])
                    value = value + decode(y_in.at[k])
            for w in ways:
                arrived(z_in.at[w, abs(zoff), y], z_recv.at[w, abs(zoff), y])
                value = value + decode(z_in.at[w, abs(zoff), y])
            if zoff == 0 and y == 1:
                grad_out[...] = value
                continue
            out = z_out.at[i]
            encode(out, value)
            if zoff == 0:
                target, place, flag = partner, y_in.at[2], y_recv.at[2]
            elif abs(zoff) == 1 and y == 0:
                target = partner_up if way == 0 else partner_down
                place, flag = y_in.at[way], y_recv.at[way]
            else:
                target = up if way == 0 else down
                near = abs(zoff) - 1
                place, flag = z_in.at[way, near, y], z_recv.at[way, near, y]
            send(out, place, z_send.at[i], flag, target, r)
        if dist == half:
            w_stage(0)
    for stage in range(w_done[0], 4):
        w_stage(stage)

    settle()


def finish(act, grad_t, wgrad, act_out, grad_out, wgrad_out):
    act_out[...] = act[...]
    wgrad_out[...] = wgrad[...]
    feat = wgrad.shape[0]
    tile = grad_t.shape[1]
    for j in range(2):
        grad_out[j * tile:(j + 1) * tile] = grad_t[j * feat:(j + 1) * feat].T


def body(features, adj_tiles, tile_counts, dst_tile, src_tile, weight, bias_term, cotangent):
    blocks = lax.axis_size("blk")
    reps = lax.axis_size("rep")
    steps, cap, tile = adj_tiles.shape[2:5]
    rows, feat = features.shape
    node_total = rows * blocks * reps
    n_slots = steps * cap
    nz = blocks // 4
    half = nz // 2
    w_rows = feat // reps
    dst = dst_tile[0, 0].T
    src = src_tile[0, 0].T
    shapes = (
        jax.ShapeDtypeStruct((rows, feat), F32),
        jax.ShapeDtypeStruct((rows, feat), F32),
        jax.ShapeDtypeStruct((feat, feat), F32),
    )
    vmem = pl.BlockSpec(memory_space=pltpu.VMEM)
    dma = pltpu.SemaphoreType.DMA
    act, grad_t, wgrad = pl.pallas_call(
        functools.partial(kernel, blocks, reps, node_total),
        out_shape=shapes,
        in_specs=[pl.BlockSpec(memory_space=pltpu.HBM)] * 8,
        out_specs=(vmem, vmem, vmem),
        scratch_shapes=[
            pltpu.SMEM((blocks,), jnp.int32),
            pltpu.SMEM((cap, blocks), jnp.int32),
            pltpu.SMEM((cap, blocks), jnp.int32),
            pltpu.VMEM((cap, blocks), jnp.int32),
            pltpu.VMEM((feat, feat), F32),
            pltpu.VMEM((1, feat), F32),
            pltpu.VMEM((rows, feat), F32),
            pltpu.VMEM((n_slots, tile, tile), BF16),
            pltpu.VMEM((blocks, rows, feat), BF16),
            pltpu.VMEM((n_slots + 1, tile, feat), F32),
            pltpu.VMEM((16, 128), jnp.int32),
            pltpu.SMEM((16, 128), jnp.int32),
            pltpu.VMEM((reps, 2, tile + SCALE_ROWS, feat), I16),
            pltpu.VMEM((reps, 2, tile + SCALE_ROWS, feat), I16),
            pltpu.VMEM((2 * reps, feat, tile), BF16),
            pltpu.VMEM((feat, feat), F32),
            pltpu.VMEM((reps, w_rows, feat), F32),
            pltpu.VMEM((4, w_rows, feat), F32),
            pltpu.VMEM((nz, w_rows, feat), F32),
            pltpu.VMEM((reps, w_rows, feat), F32),
            pltpu.VMEM((blocks // 2, 2 * feat + SCALE_ROWS, tile), I16),
            pltpu.VMEM((blocks // 2, 2 * feat + SCALE_ROWS, tile), I16),
            pltpu.VMEM((blocks // 2, 2 * feat, tile), F32),
            pltpu.VMEM((blocks // 2, 2 * feat + SCALE_ROWS, tile), I16),
            pltpu.VMEM((2, half, 2, 2 * feat + SCALE_ROWS, tile), I16),
            pltpu.VMEM((3, 2 * feat + SCALE_ROWS, tile), I16),
            dma((8,)), dma, dma,
            dma((PIECES * 2 * blocks,)), dma((blocks, PIECES)),
            dma((reps, 2)), dma((reps, 2)),
            dma((reps, 2)), dma((reps, 2)),
            dma((2 * reps + nz + 4,)), dma((reps,)), dma((4,)), dma((nz,)), dma((reps,)),
            dma((blocks // 2,)), dma((blocks // 2,)),
            dma((blocks // 2,)), dma((2, half, 2)),
            dma((3,)),
        ],
        compiler_params=pltpu.CompilerParams(
            collective_id=0, has_side_effects=True, vmem_limit_bytes=58 * 1024 * 1024
        ),
        cost_estimate=pl.CostEstimate(
            flops=4 * n_slots * tile * tile * feat,
            bytes_accessed=n_slots * tile * tile * 2,
            transcendentals=rows * feat,
        ),
        name="graph_layer",
    )(
        features, adj_tiles.reshape(n_slots, tile, tile), tile_counts[0, 0], dst, src,
        weight, bias_term.reshape(1, feat), cotangent,
    )
    return pl.pallas_call(finish, out_shape=shapes, name="outputs")(act, grad_t, wgrad)


def solution(mesh):
    in_specs = (
        P(("blk", "rep"), None),
        P("blk", "rep", None, None, None, None),
        P("blk", "rep", None),
        P("blk", "rep", None, None),
        P("blk", "rep", None, None),
        P(),
        P(),
        P(("blk", "rep"), None),
    )
    out_specs = (P(("blk", "rep"), None), P(("blk", "rep"), None), P())
    return jax.shard_map(body, mesh=mesh, in_specs=in_specs, out_specs=out_specs, check_vma=False)
```
